128 devices in a mesh: seq: 32 (over y, z, core), head: 4 (over x).
Axes of the slice: x: 4, y: 4, z: 4, core: 2. Of those that a mesh axis runs over, the one named last changes fastest.
Arguments:
- queries: bfloat16 [4096, 128, 576], P('seq', 'head'), may hold values from -400 to 400
- cache: bfloat16 [65536, 576], P('seq'), may hold values from -9 to 9
- d_out: bfloat16 [4096, 128, 512], P('seq', 'head'), may hold values from -6 to 6
- picks: int32 [4096, 6], P('seq'), may hold values from 0 to 1023, as said below
- q_pos: int32 [4096], P('seq'), may hold values from 32768 to 65535, as said below
Outputs:
- attended_out: bfloat16 [4096, 128, 512], P('seq', 'head')
- d_queries: bfloat16 [4096, 128, 576], P('seq', 'head')
- d_cache: float32 [65536, 576], P(('seq', 'head'))
The draws below stay inside these ranges and needn't reach their ends.
Inputs may be any that keep to these rules, and one draw needn't show every extreme that they name: `picks`: row q names 6 different blocks: the first holds position q_pos[q], the others lie wholly before it. The rows of one aligned run of 128 queries name at most 4 distinct blocks within one aligned range of 2048 cache tokens, and exactly 4 in some range of every draw. `q_pos`: each aligned run of 128 queries holds consecutive positions beginning at a multiple of 128.
All inputs are finite; a program needn't handle non-finite values.
Results may differ from the reference program's by a relative error of at most 0.015.
Values may be sent and summed in bfloat16 or wider, within the bound.
A program may use at most 256 MiB of HBM per device.

```python
import math
import jax
import jax.numpy as jnp
from jax import lax

D_LAT = 512
D_ROPE = 64
HEADS = 128
BLOCK = 64
NSEL = 6
POOL = 64
QDEV = 128
CTX_DEV = 2048
QN = 4096
CTX = 65536


def run_starts(key):
    key = jax.random.fold_in(key, 101)
    run_count = QN // QDEV
    chosen_runs = jax.random.randint(key, (run_count,), CTX // (2 * QDEV), CTX // QDEV)
    chosen_runs = chosen_runs.at[0].set(CTX // QDEV - 1)
    return (chosen_runs * QDEV).astype(jnp.int32)


def base_cache(key):
    key = jax.random.fold_in(key, 102)
    return jnp.clip(jax.random.normal(key, (CTX, D_LAT + D_ROPE), jnp.float32), -6.0, 6.0)


def draw_q_pos(key, part):
    run_first = run_starts(key)
    positions = run_first[:, None] + jnp.arange(QDEV, dtype=jnp.int32)[None, :]
    return positions.reshape(QN).astype(jnp.int32)


def draw_picks(key, part):
    run_first = run_starts(key)
    key = jax.random.fold_in(key, 2)
    run_count = QN // QDEV
    owner_cap = POOL // run_count
    shard_blocks = CTX_DEV // BLOCK
    key_owner, key_query = jax.random.split(key)

    def one_run(first_pos, owner_key, query_key):
        first_block = first_pos // BLOCK
        block_ids = jnp.arange(run_count * shard_blocks, dtype=jnp.int32).reshape(run_count, shard_blocks)
        raw_owner = jax.random.randint(owner_key, (run_count, shard_blocks), 0, 2 ** 20)
        owner_score = raw_owner * shard_blocks + jnp.arange(shard_blocks, dtype=jnp.int32)[None, :]
        owner_score = jnp.where(block_ids < first_block, owner_score, -1)
        best_score, best_index = lax.top_k(owner_score, owner_cap)
        pool_ids = (block_ids[:, 0:1] + best_index).reshape(POOL)
        pool_valid = (best_score >= 0).reshape(POOL)
        raw_query = jax.random.randint(query_key, (QDEV, POOL), 0, 2 ** 20)
        query_score = raw_query * POOL + jnp.arange(POOL, dtype=jnp.int32)[None, :]
        forced = jnp.arange(POOL, dtype=jnp.int32)[None, :] % QDEV == jnp.arange(QDEV, dtype=jnp.int32)[:, None]
        query_score = jnp.where(forced, query_score + 2 ** 27, query_score)
        query_score = jnp.where(pool_valid[None, :], query_score, -1)
        kept_score, kept_index = lax.top_k(query_score, NSEL - 1)
        chosen_blocks = pool_ids[kept_index]
        own_block = first_block + jnp.arange(QDEV, dtype=jnp.int32) // BLOCK
        return jnp.concatenate([own_block[:, None], chosen_blocks], axis=1)
    owner_keys = jax.random.split(key_owner, run_count)
    query_keys = jax.random.split(key_query, run_count)
    picked = jax.vmap(one_run)(run_first, owner_keys, query_keys)
    return picked.reshape(QN, NSEL).astype(jnp.int32)


def draw_cache(key, part):
    cache_rows = base_cache(key)
    return cache_rows.astype(jnp.bfloat16)


def draw_queries(key, part):
    key = jax.random.fold_in(key, 3)
    shape = (QN, HEADS, D_LAT + D_ROPE)
    query_values = jnp.clip(jax.random.normal(key, shape, jnp.float32), -6.0, 6.0)
    return query_values.astype(jnp.bfloat16)


def levels(own_key, shape, cuts, least, high):
    level, own = 1.0, jax.random.fold_in(own_key, 6)
    for position, parts in cuts:
        steps = jnp.exp(jax.random.uniform(jax.random.fold_in(own, position), (parts,), jnp.float32, least / len(cuts), high / len(cuts)))
        level = level * jnp.repeat(steps, shape[position] // parts).reshape([-1 if axis == position else 1 for axis in range(len(shape))])
    return level


def centred(own_key, dims, scale, bound, cuts=(), kind=jnp.bfloat16):
    gain = levels(own_key, dims, cuts, -0.22, 0.18) if cuts else 1.0
    entries = jax.random.normal(own_key, dims, jnp.float32) * scale * gain
    return jnp.minimum(jnp.maximum(entries, -bound), bound).astype(kind)


def setup_inputs(seed: int = 0) -> dict:
    splits = jax.random.split(jax.random.key(seed), 6)
    queries = draw_queries(jax.random.fold_in(splits[5], 71), 0)
    cache = draw_cache(jax.random.fold_in(splits[5], 71), 0)
    d_out = centred(splits[2], (QN, HEADS, D_LAT), 1.0, 6.0, ((0, 32), (1, 4)))
    picks = draw_picks(jax.random.fold_in(splits[5], 71), 0)
    q_pos = draw_q_pos(jax.random.fold_in(splits[5], 71), 0)
    return {"queries": queries, "cache": cache, "d_out": d_out, "picks": picks, "q_pos": q_pos}


score_scale = 1.0 / math.sqrt(192.0)
masked_score = -1e+30

def attend_rows(query_rows, gathered_keys, key_pos, pos_rows, grad_rows):
    lat_width = grad_rows.shape[2]
    query_full = query_rows.astype(jnp.float32)
    key_full = gathered_keys.astype(jnp.float32)
    grad_full = grad_rows.astype(jnp.float32)
    scores = jnp.einsum('bhc,bkc->bhk', query_full, key_full) * score_scale
    visible = key_pos[:, None, :] <= pos_rows[:, None, None]
    scores = jnp.where(visible, scores, masked_score)
    row_max = lax.optimization_barrier(jnp.max(scores, axis=2, keepdims=True))
    exp_scores = jnp.exp(scores - row_max)
    softmax_probs = exp_scores / lax.optimization_barrier(jnp.sum(exp_scores, axis=2, keepdims=True))
    weights = lax.optimization_barrier(softmax_probs.astype(jnp.bfloat16)).astype(jnp.float32)
    latent_values = key_full[:, :, :lat_width]
    attended = jnp.einsum('bhk,bkl->bhl', weights, latent_values)
    row_delta = lax.optimization_barrier(jnp.sum(grad_full * attended, axis=2, keepdims=True))
    d_prob = jnp.einsum('bhl,bkl->bhk', grad_full, latent_values)
    d_score = lax.optimization_barrier((softmax_probs * (d_prob - row_delta)).astype(jnp.bfloat16)).astype(jnp.float32)
    d_query = jnp.einsum('bhk,bkc->bhc', d_score, key_full) * score_scale
    d_key = jnp.einsum('bhk,bhc->bkc', d_score, query_full) * score_scale
    d_value = jnp.einsum('bhk,bhl->bkl', weights, grad_full)
    rope_zeros = jnp.zeros(d_key.shape[:2] + (d_key.shape[2] - lat_width,), jnp.float32)
    d_key = d_key + jnp.concatenate([d_value, rope_zeros], axis=2)
    return (attended.astype(jnp.bfloat16), d_query.astype(jnp.bfloat16), d_key)

def reference(queries, cache, d_out, picks, q_pos):
    query_count, head_count, key_width = queries.shape
    batch_rows = 16
    offsets = jnp.arange(BLOCK, dtype=jnp.int32)

    def attend_batch(cache_grads, first_row):
        query_rows = lax.dynamic_slice_in_dim(queries, first_row, batch_rows, 0)
        grad_rows = lax.dynamic_slice_in_dim(d_out, first_row, batch_rows, 0)
        pick_rows = lax.dynamic_slice_in_dim(picks, first_row, batch_rows, 0)
        pos_rows = lax.dynamic_slice_in_dim(q_pos, first_row, batch_rows, 0)
        key_rows = (pick_rows[:, :, None] * BLOCK + offsets[None, None, :]).reshape(batch_rows, -1).astype(jnp.int32)
        gathered_keys = jnp.take(cache, key_rows, axis=0)
        attended, d_query, d_key = attend_rows(query_rows, gathered_keys, key_rows, pos_rows, grad_rows)
        cache_grads = cache_grads.at[key_rows.reshape(-1)].add(d_key.reshape(-1, key_width))
        return (cache_grads, (attended, d_query))
    starts = jnp.arange(query_count // batch_rows, dtype=jnp.int32) * batch_rows
    d_cache, (outputs, d_queries) = lax.scan(attend_batch, jnp.zeros((CTX, key_width), jnp.float32), starts)
    outputs = outputs.reshape(query_count, head_count, -1)
    d_queries = d_queries.reshape(query_count, head_count, key_width)
    return (outputs, d_queries, d_cache)
```

```python
import functools
import math

import jax
import jax.numpy as jnp
from jax import lax
from jax.experimental import pallas as pl
from jax.experimental.pallas import tpu as pltpu
from jax.sharding import PartitionSpec as P

BLOCK = 64
POOL = 64
NSEL = 6

score_scale = 1.0 / math.sqrt(192.0)
masked_score = -1e30

BF16 = jnp.bfloat16
F32 = jnp.float32
COPY_ROWS = 16
STEP_ROWS = 8
CHUNK = 8
HBM = pl.BlockSpec(memory_space=pl.ANY)
SMEM = pl.BlockSpec(memory_space=pltpu.SMEM)
VMEM = pl.BlockSpec(memory_space=pltpu.VMEM)
VMEM_BYTES = 60 * 2**20


def take_blocks_kernel(index_ref, src, dst, sems):
    def copy(i):
        return pltpu.make_async_copy(src.at[index_ref[i]], dst.at[i], sems.at[i])

    def start(i, c):
        copy(i).start()
        return c

    def wait(i, c):
        copy(i).wait()
        return c

    lax.fori_loop(0, dst.shape[0], start, 0)
    lax.fori_loop(0, dst.shape[0], wait, 0)


def take_blocks(index, blocks):
    count = index.shape[0]
    return pl.pallas_call(
        take_blocks_kernel,
        out_shape=jax.ShapeDtypeStruct((count,) + blocks.shape[1:], blocks.dtype),
        in_specs=[SMEM, VMEM],
        out_specs=HBM,
        scratch_shapes=[pltpu.SemaphoreType.DMA((count,))],
        compiler_params=pltpu.CompilerParams(vmem_limit_bytes=VMEM_BYTES),
        name="take_blocks",
    )(index, blocks)


def add_blocks_kernel(asked_ref, src, out, total):
    total[...] = jnp.zeros_like(total)

    def add(i, c):
        block = asked_ref[i]

        @pl.when(block >= 0)
        def _():
            total[block] += src[i].astype(F32)

        return c

    lax.fori_loop(0, src.shape[0], add, 0)
    out[...] = total[...].astype(out.dtype)


def add_blocks(asked, returned, blocks_dev):
    shape = (blocks_dev,) + returned.shape[1:]
    return pl.pallas_call(
        add_blocks_kernel,
        out_shape=jax.ShapeDtypeStruct(shape, BF16),
        in_specs=[SMEM, VMEM],
        out_specs=VMEM,
        scratch_shapes=[pltpu.VMEM(shape, F32)],
        compiler_params=pltpu.CompilerParams(vmem_limit_bytes=VMEM_BYTES),
        name="add_blocks",
    )(asked, returned)


def attend_kernel(
    count_ref, slot_ref, limit_ref, q_hbm, g_hbm, k1_hbm, k2_hbm,
    o_hbm, dq_hbm, dk1_hbm, dk2_hbm,
    q_v, g_v, k_v, o_v, dq_v, dk_v, y_v, kt_v, acc_v, cnt, lst,
    sem_in, sem_k, sem_out, sem_dk,
):
    rows, heads, width = q_v.shape
    lat = g_v.shape[2]
    parts, places = k_v.shape[0], k_v.shape[1]
    near = k1_hbm.shape[1]
    groups = rows // COPY_ROWS
    slots = parts * places
    more = count_ref[0] > parts * near

    def in_copies(i):
        s = pl.ds(i * COPY_ROWS, COPY_ROWS)
        return (
            pltpu.make_async_copy(q_hbm.at[s], q_v.at[s], sem_in.at[i, 0]),
            pltpu.make_async_copy(g_hbm.at[s], g_v.at[s], sem_in.at[i, 1]),
        )

    def out_copies(i):
        s = pl.ds(i * COPY_ROWS, COPY_ROWS)
        b = lax.rem(i, 2)
        return (
            pltpu.make_async_copy(o_v.at[b], o_hbm.at[s], sem_out.at[b, 0]),
            pltpu.make_async_copy(dq_v.at[b], dq_hbm.at[s], sem_out.at[b, 1]),
        )

    key_copies = [
        pltpu.make_async_copy(k1_hbm.at[h], k_v.at[h, pl.ds(0, near)], sem_k.at[h])
        for h in range(parts)
    ]
    far_copies = [
        pltpu.make_async_copy(
            k2_hbm.at[h], k_v.at[h, pl.ds(near, places - near)], sem_k.at[parts + h]
        )
        for h in range(parts)
    ]
    for c in key_copies:
        c.start()

    @pl.when(more)
    def _():
        for c in far_copies:
            c.start()

    for i in range(groups):
        for c in in_copies(i):
            c.start()

    def clear(i, c):
        cnt[i] = 0
        return c

    lax.fori_loop(0, slots, clear, 0)
    y_v[rows * NSEL] = jnp.zeros((heads, 2 * BLOCK), BF16)
    for c in key_copies:
        c.wait()

    @pl.when(more)
    def _():
        for c in far_copies:
            c.wait()

    used = jnp.where(more, places, near)

    def turn(place, c):
        for h in range(parts):
            k = k_v[h, place]
            kt_v[place * parts + h] = jnp.concatenate([k, k], 0).T
        return c

    lax.fori_loop(0, used, turn, 0)

    lane = lax.broadcasted_iota(jnp.int32, (1, BLOCK), 1)
    low = lax.broadcasted_iota(jnp.int32, (width, 2 * BLOCK), 1) < BLOCK

    def step(at, group):
        first = group * COPY_ROWS + at * STEP_ROWS
        buf = lax.rem(group, 2)
        products, keys = [], []
        for i in range(STEP_ROWS):
            q = first + i
            picked, turned = [], []
            for j in range(NSEL):
                s = slot_ref[q * NSEL + j]
                c = cnt[s]
                lst[s * rows + c] = q * 8 + j
                cnt[s] = c + 1
                picked.append(k_v[s & 3, s >> 2])
                turned.append(kt_v[s])
            k = jnp.concatenate(picked, 0)
            kt = jnp.concatenate(
                [jnp.where(low, turned[j], turned[j + 1]) for j in range(0, NSEL, 2)], 1
            )
            grad = jnp.concatenate([g_v[q], jnp.zeros((heads, width - lat), BF16)], 1)
            both = jnp.concatenate([q_v[q], grad], 0)
            products.append(jnp.dot(both, kt, preferred_element_type=F32))
            keys.append(k)
        for i in range(STEP_ROWS):
            q = first + i
            scores = products[i][:heads] * score_scale
            d_prob = products[i][heads:]
            own = jnp.where(lane <= limit_ref[q], scores[:, :BLOCK], masked_score)
            scores = jnp.concatenate([own, scores[:, BLOCK:]], 1)
            e = jnp.exp(scores - jnp.max(scores, axis=1, keepdims=True))
            probs = e * (1.0 / jnp.sum(e, axis=1, keepdims=True))
            weights = probs.astype(BF16)
            delta = jnp.sum(weights.astype(F32) * d_prob, axis=1, keepdims=True)
            d_score = (probs * (d_prob - delta) * score_scale).astype(BF16)
            for j in range(NSEL):
                t = slice(j * BLOCK, (j + 1) * BLOCK)
                y_v[q * NSEL + j] = jnp.concatenate([d_score[:, t], weights[:, t]], 1)
            out = jnp.dot(
                jnp.concatenate([d_score, weights], 0), keys[i], preferred_element_type=F32
            )
            dq_v[buf, at * STEP_ROWS + i] = out[:heads].astype(BF16)
            o_v[buf, at * STEP_ROWS + i] = out[heads:, :lat].astype(BF16)
        return group

    def group(i, c):
        for x in in_copies(i):
            x.wait()

        @pl.when(i >= 2)
        def _():
            for x in out_copies(i - 2):
                x.wait()

        lax.fori_loop(0, COPY_ROWS // STEP_ROWS, step, i)
        for x in out_copies(i):
            x.start()
        return c

    lax.fori_loop(0, groups, group, 0)

    def key_step(place):
        names = [place * parts + h for h in range(parts)]
        counts = [cnt[s] for s in names]
        most = functools.reduce(jnp.maximum, counts)

        def chunk(c):
            sums = []
            for s, n in zip(names, counts):
                ys, qs, gs = [], [], []
                for i in range(CHUNK):
                    at = c * CHUNK + i
                    v = lst[s * rows + jnp.minimum(at, rows - 1)]
                    v = jnp.where(at < n, v, rows * 8)
                    q = v >> 3
                    ys.append(y_v[q * NSEL + (v & 7)])
                    q = jnp.minimum(q, rows - 1)
                    qs.append(q_v[q])
                    gs.append(g_v[q])
                y = jnp.concatenate(ys, 0).T
                a = jnp.dot(y[:BLOCK], jnp.concatenate(qs, 0), preferred_element_type=F32)
                b = jnp.dot(y[BLOCK:], jnp.concatenate(gs, 0), preferred_element_type=F32)
                sums.append(jnp.concatenate([a[:, :lat] + b, a[:, lat:]], 1))
            return sums

        for h, r in enumerate(chunk(0)):
            acc_v[h] = r

        def again(c, x):
            for h, r in enumerate(chunk(c)):
                acc_v[h] += r
            return x

        lax.fori_loop(1, (most + CHUNK - 1) // CHUNK, again, 0)

    def key_loop(begin, end, dk_hbm):
        def dk_copy(place):
            b = lax.rem(place, 2)
            return pltpu.make_async_copy(dk_v.at[b], dk_hbm.at[:, place - begin], sem_dk.at[b])

        def body(place, c):
            key_step(place)

            @pl.when(place >= begin + 2)
            def _():
                dk_copy(place - 2).wait()

            dk_v[lax.rem(place, 2)] = acc_v[...].astype(BF16)
            dk_copy(place).start()
            return c

        lax.fori_loop(begin, end, body, 0)
        dk_copy(jnp.int32(end - 2)).wait()
        dk_copy(jnp.int32(end - 1)).wait()

    key_loop(0, near, dk1_hbm)

    @pl.when(more)
    def _():
        key_loop(near, places, dk2_hbm)

    for i in (groups - 2, groups - 1):
        for c in out_copies(jnp.int32(i)):
            c.wait()


def attend(count, slots, limit, queries, d_out, k1, k2):
    rows, heads, width = queries.shape
    lat = d_out.shape[2]
    parts, near = k1.shape[:2]
    places = near + k2.shape[1]
    groups = rows // COPY_ROWS
    return pl.pallas_call(
        attend_kernel,
        out_shape=(
            jax.ShapeDtypeStruct((rows, heads, lat), BF16),
            jax.ShapeDtypeStruct((rows, heads, width), BF16),
            jax.ShapeDtypeStruct(k1.shape, BF16),
            jax.ShapeDtypeStruct(k2.shape, BF16),
        ),
        in_specs=[SMEM, SMEM, SMEM, HBM, HBM, HBM, HBM],
        out_specs=(HBM, HBM, HBM, HBM),
        scratch_shapes=[
            pltpu.VMEM((rows, heads, width), BF16),
            pltpu.VMEM((rows, heads, lat), BF16),
            pltpu.VMEM((parts, places, BLOCK, width), BF16),
            pltpu.VMEM((2, COPY_ROWS, heads, lat), BF16),
            pltpu.VMEM((2, COPY_ROWS, heads, width), BF16),
            pltpu.VMEM((2, parts, BLOCK, width), BF16),
            pltpu.VMEM((rows * NSEL + 1, heads, 2 * BLOCK), BF16),
            pltpu.VMEM((parts * places, width, 2 * BLOCK), BF16),
            pltpu.VMEM((parts, BLOCK, width), F32),
            pltpu.SMEM((parts * places,), jnp.int32),
            pltpu.SMEM((parts * places * rows,), jnp.int32),
            pltpu.SemaphoreType.DMA((groups, 2)),
            pltpu.SemaphoreType.DMA((2 * parts,)),
            pltpu.SemaphoreType.DMA((2, 2)),
            pltpu.SemaphoreType.DMA((2,)),
        ],
        compiler_params=pltpu.CompilerParams(vmem_limit_bytes=VMEM_BYTES),
        name="attend",
    )(count, slots, limit, queries, d_out, k1, k2)


def on_device(queries, cache, d_out, picks, q_pos):
    seq_count = lax.axis_size("seq")
    parts = lax.axis_size("head")
    part = lax.axis_index("head")
    rows, heads, width = queries.shape
    blocks_dev = cache.shape[0] // BLOCK
    all_blocks = seq_count * blocks_dev
    most_blocks = seq_count * 4
    places = most_blocks // parts
    near = -(-(POOL + rows // BLOCK) // parts)

    flat = picks.reshape(-1)
    block_ids = jnp.arange(all_blocks, dtype=jnp.int32)
    matches = flat[:, None] == block_ids[None, :]
    present = jnp.any(matches, axis=0)
    rank = jnp.cumsum(present.astype(jnp.int32)) - 1
    count = rank[-1] + 1
    slots = jnp.sum(jnp.where(matches, rank[None, :], 0), axis=1)
    mine = (present & (rank % parts == part)).reshape(seq_count, blocks_dev)
    wanted = jnp.max(
        jnp.where(mine, jnp.arange(blocks_dev, dtype=jnp.int32)[None, :], -1), axis=1
    )
    place_of = jnp.max(
        jnp.where(mine, rank.reshape(seq_count, blocks_dev) // parts, 0), axis=1
    )
    at_place = present[None, :] & (
        rank[None, :] == (jnp.arange(places, dtype=jnp.int32) * parts + part)[:, None]
    )
    owner_at = jnp.max(jnp.where(at_place, (block_ids // blocks_dev)[None, :], 0), axis=1)

    request = jnp.stack([wanted, jnp.full((seq_count,), count, jnp.int32)], axis=1)
    asked = lax.all_to_all(request, "seq", split_axis=0, concat_axis=0, tiled=True)
    blocks_asked = asked[:, 0]
    overflow = jnp.max(asked[:, 1]) > near * parts

    served = take_blocks(
        jnp.maximum(blocks_asked, 0), cache.reshape(blocks_dev, BLOCK, width)
    )
    fetched = lax.all_to_all(served, "seq", split_axis=0, concat_axis=0, tiled=True)
    compact = take_blocks(owner_at, fetched)
    k1 = lax.all_gather(compact[:near], "head", axis=0, tiled=False)
    far_shape = (parts, places - near, BLOCK, width)
    k2 = lax.cond(
        overflow,
        lambda x: lax.all_gather(x, "head", axis=0, tiled=False),
        lambda x: jnp.zeros(far_shape, BF16),
        compact[near:],
    )
    out, d_queries, dk1, dk2 = attend(
        count[None], slots, q_pos % BLOCK, queries, d_out, k1, k2
    )
    r1 = lax.psum_scatter(dk1, "head", scatter_dimension=0, tiled=False)
    r2 = lax.cond(
        overflow,
        lambda x: lax.psum_scatter(x, "head", scatter_dimension=0, tiled=False),
        lambda x: jnp.zeros(far_shape[1:], BF16),
        dk2,
    )
    back = take_blocks(place_of, jnp.concatenate([r1, r2], axis=0))
    returned = lax.all_to_all(back, "seq", split_axis=0, concat_axis=0, tiled=True)
    owned = add_blocks(blocks_asked, returned, blocks_dev)
    d_cache = lax.psum_scatter(
        owned.reshape(blocks_dev * BLOCK, width), "head", scatter_dimension=0, tiled=True
    ).astype(F32)
    return (out, d_queries, d_cache)


def solution(mesh):
    placed = (
        P("seq", "head", None),
        P("seq", None),
        P("seq", "head", None),
        P("seq", None),
        P("seq"),
    )
    return jax.shard_map(
        on_device,
        mesh=mesh,
        in_specs=placed,
        out_specs=(P("seq", "head", None), P("seq", "head", None), P(("seq", "head"), None)),
        check_vma=False,
    )
```

```python
import functools
import math

import jax
import jax.numpy as jnp
from jax import lax
from jax.experimental import pallas as pl
from jax.experimental.pallas import tpu as pltpu
from jax.sharding import PartitionSpec as P

BLOCK = 64
POOL = 64
NSEL = 6

score_scale = 1.0 / math.sqrt(192.0)
masked_score = -1e30

BF16 = jnp.bfloat16
F32 = jnp.float32
COPY_ROWS = 16
STEP_ROWS = 8
CHUNK = 8
HBM = pl.BlockSpec(memory_space=pl.ANY)
SMEM = pl.BlockSpec(memory_space=pltpu.SMEM)
VMEM = pl.BlockSpec(memory_space=pltpu.VMEM)
VMEM_BYTES = 60 * 2**20
CHUNKS = 4
MESH = pl.DeviceIdType.MESH


def take_blocks_kernel(index_ref, src, dst, sems):
    def copy(i):
        return pltpu.make_async_copy(src.at[index_ref[i]], dst.at[i], sems.at[i])

    def start(i, c):
        copy(i).start()
        return c

    def wait(i, c):
        copy(i).wait()
        return c

    lax.fori_loop(0, dst.shape[0], start, 0)
    lax.fori_loop(0, dst.shape[0], wait, 0)


def take_blocks(index, blocks):
    count = index.shape[0]
    return pl.pallas_call(
        take_blocks_kernel,
        out_shape=jax.ShapeDtypeStruct((count,) + blocks.shape[1:], blocks.dtype),
        in_specs=[SMEM, VMEM],
        out_specs=HBM,
        scratch_shapes=[pltpu.SemaphoreType.DMA((count,))],
        compiler_params=pltpu.CompilerParams(vmem_limit_bytes=VMEM_BYTES),
        name="take_blocks",
    )(index, blocks)


def unset_kernel(after_ref, out):
    del after_ref, out


def unset(after, shape):
    return pl.pallas_call(
        unset_kernel,
        out_shape=jax.ShapeDtypeStruct(shape, BF16),
        in_specs=[HBM],
        out_specs=HBM,
        name="unset",
    )(after)


def fetch_kernel(asked_ref, owner_ref, cache_v, near_hbm, all_hbm,
                 send_v, recv, pack_v, a_send, a_recv, x_send, x_recv, own_sem, all_sem):
    chunks, seq_count, rows, _ = send_v.shape
    near = pack_v.shape[1]
    parts = near_hbm.shape[1]
    cut = (near + 1) // 2
    me, part = lax.axis_index("seq"), lax.axis_index("head")
    right, left = lax.rem(part + 1, parts), lax.rem(part + parts - 1, parts)
    barrier = pltpu.get_barrier_semaphore()

    def greet(d, c):
        peer = lax.rem(me + d, seq_count)
        pl.semaphore_signal(barrier, inc=1, device_id=(peer, part), device_id_type=MESH)
        return c

    lax.fori_loop(1, seq_count, greet, 0)
    for x in (left, right):
        pl.semaphore_signal(barrier, inc=1, device_id=(me, x), device_id_type=MESH)
    for c in range(chunks):

        def serve(p, x, c=c):
            send_v[c, p] = cache_v[asked_ref[p], c * rows : (c + 1) * rows]
            return x

        lax.fori_loop(0, seq_count, serve, 0)
    pl.semaphore_wait(barrier, seq_count + 1)
    for c in range(chunks):

        def send(d, x, c=c):
            peer = lax.rem(me + d, seq_count)
            pltpu.make_async_remote_copy(
                src_ref=send_v.at[c, peer], dst_ref=recv[c].at[me],
                send_sem=a_send.at[c], recv_sem=a_recv.at[c],
                device_id=(peer, part), device_id_type=MESH,
            ).start()
            return x

        lax.fori_loop(1, seq_count, send, 0)
        recv[c][me] = send_v[c, me]

    def over_x(c, way, src, dst, to):
        return pltpu.make_async_remote_copy(
            src_ref=src, dst_ref=dst, send_sem=x_send.at[c, way], recv_sem=x_recv.at[c, way],
            device_id=(me, to), device_id_type=MESH,
        )

    def direct(c):
        out = near_hbm.at[c, part]
        return (over_x(c, 0, pack_v.at[c], out, right), over_x(c, 1, pack_v.at[c], out, left))

    def onward(c):
        one = near_hbm.at[c, left, pl.ds(0, cut)]
        two = near_hbm.at[c, right, pl.ds(cut, near - cut)]
        return (over_x(c, 2, one, one, right), over_x(c, 3, two, two, left))

    def own(c):
        return pltpu.make_async_copy(pack_v.at[c], near_hbm.at[c, part], own_sem.at[c])

    def keep(c):
        return pltpu.make_async_copy(recv[c], all_hbm.at[c], all_sem.at[c])

    def forward(c):
        for x, y in zip(direct(c), onward(c)):
            x.wait_recv()
            y.start()

    for c in range(chunks):
        whole = recv[c].at[pl.ds(0, seq_count - 1)]
        pltpu.make_async_copy(whole, whole, a_recv.at[c]).wait()

        def pack(i, x, c=c):
            pack_v[c, i] = recv[c][owner_ref[i]]
            return x

        lax.fori_loop(0, near, pack, 0)
        for x in direct(c):
            x.start()
        own(c).start()
        keep(c).start()
        if c:
            forward(c - 1)
    forward(chunks - 1)
    for c in range(chunks):
        whole = send_v.at[c, pl.ds(0, seq_count - 1)]
        pltpu.make_async_copy(whole, whole, a_send.at[c]).wait()
        own(c).wait()
        keep(c).wait()
        for x, y in zip(direct(c), onward(c)):
            x.wait_send()
            y.wait_send()
            y.wait_recv()


def fetch(asked, owner_at, blocks, near, parts):
    seq_count = asked.shape[0]
    width = blocks.shape[2]
    rows = BLOCK // CHUNKS
    dma = pltpu.SemaphoreType.DMA
    return pl.pallas_call(
        fetch_kernel,
        out_shape=(
            jax.ShapeDtypeStruct((CHUNKS, parts, near, rows, width), BF16),
            jax.ShapeDtypeStruct((CHUNKS, seq_count, rows, width), BF16),
        ),
        in_specs=[SMEM, SMEM, VMEM],
        out_specs=(HBM, HBM),
        scratch_shapes=[
            pltpu.VMEM((CHUNKS, seq_count, rows, width), BF16),
            [pltpu.VMEM((seq_count, rows, width), BF16)] * CHUNKS,
            pltpu.VMEM((CHUNKS, near, rows, width), BF16),
            dma((CHUNKS,)), dma((CHUNKS,)), dma((CHUNKS, 4)), dma((CHUNKS, 4)),
            dma((CHUNKS,)), dma((CHUNKS,)),
        ],
        compiler_params=pltpu.CompilerParams(
            vmem_limit_bytes=VMEM_BYTES, collective_id=1, has_side_effects=True
        ),
        name="fetch",
    )(asked, owner_at, blocks)


def add_blocks_kernel(asked_ref, src, out, total):
    total[...] = jnp.zeros_like(total)

    def add(i, c):
        block = asked_ref[i]

        @pl.when(block >= 0)
        def _():
            total[block] += src[i].astype(F32)

        return c

    lax.fori_loop(0, src.shape[0], add, 0)
    out[...] = total[...].astype(out.dtype)


def add_blocks(asked, returned, blocks_dev):
    shape = (blocks_dev,) + returned.shape[1:]
    return pl.pallas_call(
        add_blocks_kernel,
        out_shape=jax.ShapeDtypeStruct(shape, BF16),
        in_specs=[SMEM, VMEM],
        out_specs=VMEM,
        scratch_shapes=[pltpu.VMEM(shape, F32)],
        compiler_params=pltpu.CompilerParams(vmem_limit_bytes=VMEM_BYTES),
        name="add_blocks",
    )(asked, returned)


def attend_kernel(
    count_ref, slot_ref, limit_ref, q_hbm, g_hbm, k1_hbm, k2_hbm,
    o_hbm, dq_hbm, dk1_hbm, dk2_hbm,
    q_v, g_v, k_v, o_v, dq_v, dk_v, y_v, kt_v, acc_v, cnt, lst,
    sem_in, sem_k, sem_out, sem_dk,
):
    rows, heads, width = q_v.shape
    lat = g_v.shape[2]
    parts, places = k_v.shape[0], k_v.shape[1]
    chunks, _, near, piece, _ = k1_hbm.shape
    groups = rows // COPY_ROWS
    slots = parts * places
    more = count_ref[0] > parts * near

    def in_copies(i):
        s = pl.ds(i * COPY_ROWS, COPY_ROWS)
        return (
            pltpu.make_async_copy(q_hbm.at[s], q_v.at[s], sem_in.at[i, 0]),
            pltpu.make_async_copy(g_hbm.at[s], g_v.at[s], sem_in.at[i, 1]),
        )

    def out_copies(i):
        s = pl.ds(i * COPY_ROWS, COPY_ROWS)
        b = lax.rem(i, 2)
        return (
            pltpu.make_async_copy(o_v.at[b], o_hbm.at[s], sem_out.at[b, 0]),
            pltpu.make_async_copy(dq_v.at[b], dq_hbm.at[s], sem_out.at[b, 1]),
        )

    key_copies = [
        pltpu.make_async_copy(
            k1_hbm.at[c, h], k_v.at[h, pl.ds(0, near), pl.ds(c * piece, piece)], sem_k.at[c, h]
        )
        for c in range(chunks)
        for h in range(parts)
    ]
    far_copies = [
        pltpu.make_async_copy(
            k2_hbm.at[h], k_v.at[h, pl.ds(near, places - near)], sem_k.at[chunks, h]
        )
        for h in range(parts)
    ]
    for c in key_copies:
        c.start()

    @pl.when(more)
    def _():
        for c in far_copies:
            c.start()

    for i in range(groups):
        for c in in_copies(i):
            c.start()

    def clear(i, c):
        cnt[i] = 0
        return c

    lax.fori_loop(0, slots, clear, 0)
    y_v[rows * NSEL] = jnp.zeros((heads, 2 * BLOCK), BF16)
    for c in key_copies:
        c.wait()

    @pl.when(more)
    def _():
        for c in far_copies:
            c.wait()

    used = jnp.where(more, places, near)

    def turn(place, c):
        for h in range(parts):
            k = k_v[h, place]
            kt_v[place * parts + h] = jnp.concatenate([k, k], 0).T
        return c

    lax.fori_loop(0, used, turn, 0)

    lane = lax.broadcasted_iota(jnp.int32, (1, BLOCK), 1)
    low = lax.broadcasted_iota(jnp.int32, (width, 2 * BLOCK), 1) < BLOCK

    def step(at, group):
        first = group * COPY_ROWS + at * STEP_ROWS
        buf = lax.rem(group, 2)
        products, keys = [], []
        for i in range(STEP_ROWS):
            q = first + i
            picked, turned = [], []
            for j in range(NSEL):
                s = slot_ref[q * NSEL + j]
                c = cnt[s]
                lst[s * rows + c] = q * 8 + j
                cnt[s] = c + 1
                picked.append(k_v[s & 3, s >> 2])
                turned.append(kt_v[s])
            k = jnp.concatenate(picked, 0)
            kt = jnp.concatenate(
                [jnp.where(low, turned[j], turned[j + 1]) for j in range(0, NSEL, 2)], 1
            )
            grad = jnp.concatenate([g_v[q], jnp.zeros((heads, width - lat), BF16)], 1)
            both = jnp.concatenate([q_v[q], grad], 0)
            products.append(jnp.dot(both, kt, preferred_element_type=F32))
            keys.append(k)
        for i in range(STEP_ROWS):
            q = first + i
            scores = products[i][:heads] * score_scale
            d_prob = products[i][heads:]
            own = jnp.where(lane <= limit_ref[q], scores[:, :BLOCK], masked_score)
            scores = jnp.concatenate([own, scores[:, BLOCK:]], 1)
            e = jnp.exp(scores - jnp.max(scores, axis=1, keepdims=True))
            probs = e * (1.0 / jnp.sum(e, axis=1, keepdims=True))
            weights = probs.astype(BF16)
            delta = jnp.sum(weights.astype(F32) * d_prob, axis=1, keepdims=True)
            d_score = (probs * (d_prob - delta) * score_scale).astype(BF16)
            for j in range(NSEL):
                t = slice(j * BLOCK, (j + 1) * BLOCK)
                y_v[q * NSEL + j] = jnp.concatenate([d_score[:, t], weights[:, t]], 1)
            out = jnp.dot(
                jnp.concatenate([d_score, weights], 0), keys[i], preferred_element_type=F32
            )
            dq_v[buf, at * STEP_ROWS + i] = out[:heads].astype(BF16)
            o_v[buf, at * STEP_ROWS + i] = out[heads:, :lat].astype(BF16)
        return group

    def group(i, c):
        for x in in_copies(i):
            x.wait()

        @pl.when(i >= 2)
        def _():
            for x in out_copies(i - 2):
                x.wait()

        lax.fori_loop(0, COPY_ROWS // STEP_ROWS, step, i)
        for x in out_copies(i):
            x.start()
        return c

    lax.fori_loop(0, groups, group, 0)

    def key_step(place):
        names = [place * parts + h for h in range(parts)]
        counts = [cnt[s] for s in names]
        most = functools.reduce(jnp.maximum, counts)

        def chunk(c):
            sums = []
            for s, n in zip(names, counts):
                ys, qs, gs = [], [], []
                for i in range(CHUNK):
                    at = c * CHUNK + i
                    v = lst[s * rows + jnp.minimum(at, rows - 1)]
                    v = jnp.where(at < n, v, rows * 8)
                    q = v >> 3
                    ys.append(y_v[q * NSEL + (v & 7)])
                    q = jnp.minimum(q, rows - 1)
                    qs.append(q_v[q])
                    gs.append(g_v[q])
                y = jnp.concatenate(ys, 0).T
                a = jnp.dot(y[:BLOCK], jnp.concatenate(qs, 0), preferred_element_type=F32)
                b = jnp.dot(y[BLOCK:], jnp.concatenate(gs, 0), preferred_element_type=F32)
                sums.append(jnp.concatenate([a[:, :lat] + b, a[:, lat:]], 1))
            return sums

        for h, r in enumerate(chunk(0)):
            acc_v[h] = r

        def again(c, x):
            for h, r in enumerate(chunk(c)):
                acc_v[h] += r
            return x

        lax.fori_loop(1, (most + CHUNK - 1) // CHUNK, again, 0)

    def key_loop(begin, end, dk_hbm):
        def dk_copy(place):
            b = lax.rem(place, 2)
            return pltpu.make_async_copy(dk_v.at[b], dk_hbm.at[:, place - begin], sem_dk.at[b])

        def body(place, c):
            key_step(place)

            @pl.when(place >= begin + 2)
            def _():
                dk_copy(place - 2).wait()

            dk_v[lax.rem(place, 2)] = acc_v[...].astype(BF16)
            dk_copy(place).start()
            return c

        lax.fori_loop(begin, end, body, 0)
        dk_copy(jnp.int32(end - 2)).wait()
        dk_copy(jnp.int32(end - 1)).wait()

    key_loop(0, near, dk1_hbm)

    @pl.when(more)
    def _():
        key_loop(near, places, dk2_hbm)

    for i in (groups - 2, groups - 1):
        for c in out_copies(jnp.int32(i)):
            c.wait()


def attend(count, slots, limit, queries, d_out, k1, k2):
    rows, heads, width = queries.shape
    lat = d_out.shape[2]
    parts, near = k1.shape[1:3]
    places = near + k2.shape[1]
    groups = rows // COPY_ROWS
    return pl.pallas_call(
        attend_kernel,
        out_shape=(
            jax.ShapeDtypeStruct((rows, heads, lat), BF16),
            jax.ShapeDtypeStruct((rows, heads, width), BF16),
            jax.ShapeDtypeStruct((parts, near, BLOCK, width), BF16),
            jax.ShapeDtypeStruct(k2.shape, BF16),
        ),
        in_specs=[SMEM, SMEM, SMEM, HBM, HBM, HBM, HBM],
        out_specs=(HBM, HBM, HBM, HBM),
        scratch_shapes=[
            pltpu.VMEM((rows, heads, width), BF16),
            pltpu.VMEM((rows, heads, lat), BF16),
            pltpu.VMEM((parts, places, BLOCK, width), BF16),
            pltpu.VMEM((2, COPY_ROWS, heads, lat), BF16),
            pltpu.VMEM((2, COPY_ROWS, heads, width), BF16),
            pltpu.VMEM((2, parts, BLOCK, width), BF16),
            pltpu.VMEM((rows * NSEL + 1, heads, 2 * BLOCK), BF16),
            pltpu.VMEM((parts * places, width, 2 * BLOCK), BF16),
            pltpu.VMEM((parts, BLOCK, width), F32),
            pltpu.SMEM((parts * places,), jnp.int32),
            pltpu.SMEM((parts * places * rows,), jnp.int32),
            pltpu.SemaphoreType.DMA((groups, 2)),
            pltpu.SemaphoreType.DMA((CHUNKS + 1, parts)),
            pltpu.SemaphoreType.DMA((2, 2)),
            pltpu.SemaphoreType.DMA((2,)),
        ],
        compiler_params=pltpu.CompilerParams(vmem_limit_bytes=VMEM_BYTES),
        name="attend",
    )(count, slots, limit, queries, d_out, k1, k2)


def on_device(queries, cache, d_out, picks, q_pos):
    seq_count = lax.axis_size("seq")
    parts = lax.axis_size("head")
    part = lax.axis_index("head")
    rows, heads, width = queries.shape
    blocks_dev = cache.shape[0] // BLOCK
    all_blocks = seq_count * blocks_dev
    most_blocks = seq_count * 4
    places = most_blocks // parts
    near = -(-(POOL + rows // BLOCK) // parts)

    flat = picks.reshape(-1)
    block_ids = jnp.arange(all_blocks, dtype=jnp.int32)
    matches = flat[:, None] == block_ids[None, :]
    present = jnp.any(matches, axis=0)
    rank = jnp.cumsum(present.astype(jnp.int32)) - 1
    count = rank[-1] + 1
    slots = jnp.sum(jnp.where(matches, rank[None, :], 0), axis=1)
    mine = (present & (rank % parts == part)).reshape(seq_count, blocks_dev)
    wanted = jnp.max(
        jnp.where(mine, jnp.arange(blocks_dev, dtype=jnp.int32)[None, :], -1), axis=1
    )
    place_of = jnp.max(
        jnp.where(mine, rank.reshape(seq_count, blocks_dev) // parts, 0), axis=1
    )
    at_place = present[None, :] & (
        rank[None, :] == (jnp.arange(places, dtype=jnp.int32) * parts + part)[:, None]
    )
    owner_at = jnp.max(jnp.where(at_place, (block_ids // blocks_dev)[None, :], 0), axis=1)

    request = jnp.stack([wanted, jnp.full((seq_count,), count, jnp.int32)], axis=1)
    asked = lax.all_to_all(request, "seq", split_axis=0, concat_axis=0, tiled=True)
    blocks_asked = asked[:, 0]
    overflow = jnp.max(asked[:, 1]) > near * parts

    k1, fetched = fetch(
        jnp.maximum(blocks_asked, 0),
        owner_at[:near],
        cache.reshape(blocks_dev, BLOCK, width),
        near,
        parts,
    )
    far_shape = (parts, places - near, BLOCK, width)

    def gather_far(x):
        x = x.transpose(1, 0, 2, 3).reshape(seq_count, BLOCK, width)
        return lax.all_gather(take_blocks(owner_at[near:], x), "head", axis=0, tiled=False)

    k2 = lax.cond(overflow, gather_far, lambda x: unset(x, far_shape), fetched)
    out, d_queries, dk1, dk2 = attend(
        count[None], slots, q_pos % BLOCK, queries, d_out, k1, k2
    )
    r1 = lax.psum_scatter(dk1, "head", scatter_dimension=0, tiled=False)
    r2 = lax.cond(
        overflow,
        lambda x: lax.psum_scatter(x, "head", scatter_dimension=0, tiled=False),
        lambda x: unset(x, far_shape[1:]),
        dk2,
    )
    back = take_blocks(place_of, jnp.concatenate([r1, r2], axis=0))
    returned = lax.all_to_all(back, "seq", split_axis=0, concat_axis=0, tiled=True)
    owned = add_blocks(blocks_asked, returned, blocks_dev)
    d_cache = lax.psum_scatter(
        owned.reshape(blocks_dev * BLOCK, width), "head", scatter_dimension=0, tiled=True
    ).astype(F32)
    return (out, d_queries, d_cache)


def solution(mesh):
    placed = (
        P("seq", "head", None),
        P("seq", None),
        P("seq", "head", None),
        P("seq", None),
        P("seq"),
    )
    return jax.shard_map(
        on_device,
        mesh=mesh,
        in_specs=placed,
        out_specs=(P("seq", "head", None), P("seq", "head", None), P(("seq", "head"), None)),
        check_vma=False,
    )
```

```python
import functools
import math

import jax
import jax.numpy as jnp
from jax import lax
from jax.experimental import pallas as pl
from jax.experimental.pallas import tpu as pltpu
from jax.sharding import PartitionSpec as P

BLOCK = 64
POOL = 64
NSEL = 6

score_scale = 1.0 / math.sqrt(192.0)
masked_score = -1e30

BF16 = jnp.bfloat16
F32 = jnp.float32
COPY_ROWS = 16
STEP_ROWS = 8
CHUNK = 8
HBM = pl.BlockSpec(memory_space=pl.ANY)
SMEM = pl.BlockSpec(memory_space=pltpu.SMEM)
VMEM = pl.BlockSpec(memory_space=pltpu.VMEM)
VMEM_BYTES = 60 * 2**20
CHUNKS = 4
STRIDE = 13
MESH = pl.DeviceIdType.MESH


def take_blocks_kernel(index_ref, src, dst, sems):
    def copy(i):
        return pltpu.make_async_copy(src.at[index_ref[i]], dst.at[i], sems.at[i])

    def start(i, c):
        copy(i).start()
        return c

    def wait(i, c):
        copy(i).wait()
        return c

    lax.fori_loop(0, dst.shape[0], start, 0)
    lax.fori_loop(0, dst.shape[0], wait, 0)


def take_blocks(index, blocks):
    count = index.shape[0]
    return pl.pallas_call(
        take_blocks_kernel,
        out_shape=jax.ShapeDtypeStruct((count,) + blocks.shape[1:], blocks.dtype),
        in_specs=[SMEM, VMEM],
        out_specs=HBM,
        scratch_shapes=[pltpu.SemaphoreType.DMA((count,))],
        compiler_params=pltpu.CompilerParams(vmem_limit_bytes=VMEM_BYTES),
        name="take_blocks",
    )(index, blocks)


def unset_kernel(after_ref, out):
    del after_ref, out


def unset(after, shape):
    return pl.pallas_call(
        unset_kernel,
        out_shape=jax.ShapeDtypeStruct(shape, BF16),
        in_specs=[HBM],
        out_specs=HBM,
        name="unset",
    )(after)


def fetch_kernel(asked_ref, owner_ref, cache_v, near_hbm, all_hbm,
                 send_v, recv, pack_v, a_send, a_recv, x_send, x_recv, own_sem, all_sem):
    chunks, seq_count, rows, _ = send_v.shape
    near = pack_v.shape[1]
    parts = near_hbm.shape[1]
    cut = (near + 1) // 2
    me, part = lax.axis_index("seq"), lax.axis_index("head")
    right, left = lax.rem(part + 1, parts), lax.rem(part + parts - 1, parts)
    barrier = pltpu.get_barrier_semaphore()

    def greet(d, c):
        peer = lax.rem(me + d * STRIDE, seq_count)
        pl.semaphore_signal(barrier, inc=1, device_id=(peer, part), device_id_type=MESH)
        return c

    lax.fori_loop(1, seq_count, greet, 0)
    for x in (left, right):
        pl.semaphore_signal(barrier, inc=1, device_id=(me, x), device_id_type=MESH)
    for c in range(chunks):

        def serve(p, x, c=c):
            send_v[c, p] = cache_v[asked_ref[p], c * rows : (c + 1) * rows]
            return x

        lax.fori_loop(0, seq_count, serve, 0)
    pl.semaphore_wait(barrier, seq_count + 1)
    for c in range(chunks):

        def send(d, x, c=c):
            peer = lax.rem(me + d * STRIDE, seq_count)
            pltpu.make_async_remote_copy(
                src_ref=send_v.at[c, peer], dst_ref=recv[c].at[me],
                send_sem=a_send.at[c], recv_sem=a_recv.at[c],
                device_id=(peer, part), device_id_type=MESH,
            ).start()
            return x

        lax.fori_loop(1, seq_count, send, 0)
        recv[c][me] = send_v[c, me]

    def over_x(c, way, src, dst, to):
        return pltpu.make_async_remote_copy(
            src_ref=src, dst_ref=dst, send_sem=x_send.at[c, way], recv_sem=x_recv.at[c, way],
            device_id=(me, to), device_id_type=MESH,
        )

    def direct(c):
        out = near_hbm.at[c, part]
        return (over_x(c, 0, pack_v.at[c], out, right), over_x(c, 1, pack_v.at[c], out, left))

    def onward(c):
        one = near_hbm.at[c, left, pl.ds(0, cut)]
        two = near_hbm.at[c, right, pl.ds(cut, near - cut)]
        return (over_x(c, 2, one, one, right), over_x(c, 3, two, two, left))

    def own(c):
        return pltpu.make_async_copy(pack_v.at[c], near_hbm.at[c, part], own_sem.at[c])

    def keep(c):
        return pltpu.make_async_copy(recv[c], all_hbm.at[c], all_sem.at[c])

    def forward(c):
        for x, y in zip(direct(c), onward(c)):
            x.wait_recv()
            y.start()

    for c in range(chunks):
        whole = recv[c].at[pl.ds(0, seq_count - 1)]
        pltpu.make_async_copy(whole, whole, a_recv.at[c]).wait()

        def pack(i, x, c=c):
            pack_v[c, i] = recv[c][owner_ref[i]]
            return x

        lax.fori_loop(0, near, pack, 0)
        for x in direct(c):
            x.start()
        own(c).start()
        keep(c).start()
        if c:
            forward(c - 1)
    forward(chunks - 1)
    for c in range(chunks):
        whole = send_v.at[c, pl.ds(0, seq_count - 1)]
        pltpu.make_async_copy(whole, whole, a_send.at[c]).wait()
        own(c).wait()
        keep(c).wait()
        for x, y in zip(direct(c), onward(c)):
            x.wait_send()
            y.wait_send()
            y.wait_recv()


def fetch(asked, owner_at, blocks, near, parts):
    seq_count = asked.shape[0]
    width = blocks.shape[2]
    rows = BLOCK // CHUNKS
    dma = pltpu.SemaphoreType.DMA
    return pl.pallas_call(
        fetch_kernel,
        out_shape=(
            jax.ShapeDtypeStruct((CHUNKS, parts, near, rows, width), BF16),
            jax.ShapeDtypeStruct((CHUNKS, seq_count, rows, width), BF16),
        ),
        in_specs=[SMEM, SMEM, VMEM],
        out_specs=(HBM, HBM),
        scratch_shapes=[
            pltpu.VMEM((CHUNKS, seq_count, rows, width), BF16),
            [pltpu.VMEM((seq_count, rows, width), BF16)] * CHUNKS,
            pltpu.VMEM((CHUNKS, near, rows, width), BF16),
            dma((CHUNKS,)), dma((CHUNKS,)), dma((CHUNKS, 4)), dma((CHUNKS, 4)),
            dma((CHUNKS,)), dma((CHUNKS,)),
        ],
        compiler_params=pltpu.CompilerParams(
            vmem_limit_bytes=VMEM_BYTES, collective_id=1, has_side_effects=True
        ),
        name="fetch",
    )(asked, owner_at, blocks)


def give_back_kernel(place_ref, dk_v, far_v, out_hbm,
                     sum_r, sum_l, one_l, one_r, two_l, two_r, places_v, back_v,
                     x_send, x_recv, a_send, a_recv, own_sem):
    chunks, parts, near, rows, _ = dk_v.shape
    seq_count = back_v.shape[1]
    cut = (near + 1) // 2
    me, part = lax.axis_index("seq"), lax.axis_index("head")
    right, left = lax.rem(part + 1, parts), lax.rem(part + parts - 1, parts)
    far = lax.rem(part + 2, parts)
    barrier = pltpu.get_barrier_semaphore()

    def greet(d, c):
        peer = lax.rem(me + d * STRIDE, seq_count)
        pl.semaphore_signal(barrier, inc=1, device_id=(peer, part), device_id_type=MESH)
        return c

    lax.fori_loop(1, seq_count, greet, 0)
    for x in (left, right):
        pl.semaphore_signal(barrier, inc=1, device_id=(me, x), device_id_type=MESH)
    pl.semaphore_wait(barrier, seq_count + 1)

    def over_x(c, way, src, dst, to):
        return pltpu.make_async_remote_copy(
            src_ref=src, dst_ref=dst, send_sem=x_send.at[c, way], recv_sem=x_recv.at[c, way],
            device_id=(me, to), device_id_type=MESH,
        )

    def first(c):
        return (
            over_x(c, 0, dk_v.at[c, far, pl.ds(0, cut)], one_l.at[c], right),
            over_x(c, 1, dk_v.at[c, far, pl.ds(cut, near - cut)], one_r.at[c], left),
        )

    def second(c):
        return (
            over_x(c, 2, sum_r.at[c], two_l.at[c], right),
            over_x(c, 3, sum_l.at[c], two_r.at[c], left),
        )

    def own(c):
        return pltpu.make_async_copy(back_v.at[c, me], out_hbm.at[c, me], own_sem.at[c])

    def begin(c):
        for x in first(c):
            x.start()

    def add_far(c):
        from_left, from_right = first(c)
        to_right, to_left = second(c)
        from_left.wait_recv()
        sum_r[c, :cut] = (dk_v[c, right, :cut].astype(F32) + one_l[c].astype(F32)).astype(BF16)
        sum_r[c, cut:] = dk_v[c, right, cut:]
        to_right.start()
        from_right.wait_recv()
        sum_l[c, :cut] = dk_v[c, left, :cut]
        sum_l[c, cut:] = (dk_v[c, left, cut:].astype(F32) + one_r[c].astype(F32)).astype(BF16)
        to_left.start()

    def to_owners(c):
        for x in second(c):
            x.wait_recv()
        places_v[:near] = (
            dk_v[c, part].astype(F32) + two_l[c].astype(F32) + two_r[c].astype(F32)
        ).astype(BF16)
        places_v[near:] = far_v[:, c * rows : (c + 1) * rows]

        def place(o, x):
            back_v[c, o] = places_v[place_ref[o]]
            return x

        lax.fori_loop(0, seq_count, place, 0)

        def send(d, x):
            peer = lax.rem(me + d * STRIDE, seq_count)
            pltpu.make_async_remote_copy(
                src_ref=back_v.at[c, peer], dst_ref=out_hbm.at[c, me],
                send_sem=a_send.at[c], recv_sem=a_recv.at[c],
                device_id=(peer, part), device_id_type=MESH,
            ).start()
            return x

        lax.fori_loop(1, seq_count, send, 0)
        own(c).start()

    begin(0)
    begin(1)
    for c in range(chunks + 1):
        if c < chunks:
            add_far(c)
        if c + 2 < chunks:
            begin(c + 2)
        if c:
            to_owners(c - 1)
    for c in range(chunks):
        whole = back_v.at[c, pl.ds(0, seq_count - 1)]
        pltpu.make_async_copy(whole, whole, a_send.at[c]).wait()
        landed = out_hbm.at[c, pl.ds(0, seq_count - 1)]
        pltpu.make_async_copy(landed, landed, a_recv.at[c]).wait()
        own(c).wait()
        for x in first(c) + second(c):
            x.wait_send()


def give_back(place_of, dk, far):
    chunks, parts, near, rows, width = dk.shape
    seq_count = place_of.shape[0]
    cut = (near + 1) // 2
    dma = pltpu.SemaphoreType.DMA
    piece = [pltpu.VMEM((chunks, n, rows, width), BF16)
             for n in (near, near, cut, near - cut, near, near)]
    return pl.pallas_call(
        give_back_kernel,
        out_shape=jax.ShapeDtypeStruct((chunks, seq_count, rows, width), BF16),
        in_specs=[SMEM, VMEM, VMEM],
        out_specs=HBM,
        scratch_shapes=piece + [
            pltpu.VMEM((near + far.shape[0], rows, width), BF16),
            pltpu.VMEM((chunks, seq_count, rows, width), BF16),
            dma((chunks, 4)), dma((chunks, 4)), dma((chunks,)), dma((chunks,)), dma((chunks,)),
        ],
        compiler_params=pltpu.CompilerParams(
            vmem_limit_bytes=VMEM_BYTES, collective_id=2, has_side_effects=True
        ),
        name="give_back",
    )(place_of, dk, far)


def add_blocks_kernel(asked_ref, src, out, total):
    chunks, seq_count, rows, _ = src.shape
    total[...] = jnp.zeros_like(total)

    def add(i, x):
        block = asked_ref[i]

        @pl.when(block >= 0)
        def _():
            for c in range(chunks):
                total[block, c * rows : (c + 1) * rows] += src[c, i].astype(F32)

        return x

    lax.fori_loop(0, seq_count, add, 0)
    out[...] = total[...].astype(out.dtype)


def add_blocks(asked, returned, blocks_dev):
    shape = (blocks_dev, BLOCK, returned.shape[-1])
    return pl.pallas_call(
        add_blocks_kernel,
        out_shape=jax.ShapeDtypeStruct(shape, BF16),
        in_specs=[SMEM, VMEM],
        out_specs=VMEM,
        scratch_shapes=[pltpu.VMEM(shape, F32)],
        compiler_params=pltpu.CompilerParams(vmem_limit_bytes=VMEM_BYTES),
        name="add_blocks",
    )(asked, returned)


def attend_kernel(
    count_ref, slot_ref, limit_ref, q_hbm, g_hbm, k1_hbm, k2_hbm,
    o_hbm, dq_hbm, dk1_hbm, dk2_hbm,
    q_v, g_v, k_v, o_v, dq_v, dk_v, y_v, kt_v, acc_v, cnt, lst,
    sem_in, sem_k, sem_out, sem_dk,
):
    rows, heads, width = q_v.shape
    lat = g_v.shape[2]
    parts, places = k_v.shape[0], k_v.shape[1]
    chunks, _, near, piece, _ = k1_hbm.shape
    groups = rows // COPY_ROWS
    slots = parts * places
    more = count_ref[0] > parts * near

    def in_copies(i):
        s = pl.ds(i * COPY_ROWS, COPY_ROWS)
        return (
            pltpu.make_async_copy(q_hbm.at[s], q_v.at[s], sem_in.at[i, 0]),
            pltpu.make_async_copy(g_hbm.at[s], g_v.at[s], sem_in.at[i, 1]),
        )

    def out_copies(i):
        s = pl.ds(i * COPY_ROWS, COPY_ROWS)
        b = lax.rem(i, 2)
        return (
            pltpu.make_async_copy(o_v.at[b], o_hbm.at[s], sem_out.at[b, 0]),
            pltpu.make_async_copy(dq_v.at[b], dq_hbm.at[s], sem_out.at[b, 1]),
        )

    key_copies = [
        pltpu.make_async_copy(
            k1_hbm.at[c, h], k_v.at[h, pl.ds(0, near), pl.ds(c * piece, piece)], sem_k.at[c, h]
        )
        for c in range(chunks)
        for h in range(parts)
    ]
    far_copies = [
        pltpu.make_async_copy(
            k2_hbm.at[h], k_v.at[h, pl.ds(near, places - near)], sem_k.at[chunks, h]
        )
        for h in range(parts)
    ]
    for c in key_copies:
        c.start()

    @pl.when(more)
    def _():
        for c in far_copies:
            c.start()

    for i in range(groups):
        for c in in_copies(i):
            c.start()

    def clear(i, c):
        cnt[i] = 0
        return c

    lax.fori_loop(0, slots, clear, 0)
    y_v[rows * NSEL] = jnp.zeros((heads, 2 * BLOCK), BF16)
    for c in key_copies:
        c.wait()

    @pl.when(more)
    def _():
        for c in far_copies:
            c.wait()

    used = jnp.where(more, places, near)

    def turn(place, c):
        for h in range(parts):
            k = k_v[h, place]
            kt_v[place * parts + h] = jnp.concatenate([k, k], 0).T
        return c

    lax.fori_loop(0, used, turn, 0)

    lane = lax.broadcasted_iota(jnp.int32, (1, BLOCK), 1)
    low = lax.broadcasted_iota(jnp.int32, (width, 2 * BLOCK), 1) < BLOCK

    def step(at, group):
        first = group * COPY_ROWS + at * STEP_ROWS
        buf = lax.rem(group, 2)
        products, keys = [], []
        for i in range(STEP_ROWS):
            q = first + i
            picked, turned = [], []
            for j in range(NSEL):
                s = slot_ref[q * NSEL + j]
                c = cnt[s]
                lst[s * rows + c] = q * 8 + j
                cnt[s] = c + 1
                picked.append(k_v[s & 3, s >> 2])
                turned.append(kt_v[s])
            k = jnp.concatenate(picked, 0)
            kt = jnp.concatenate(
                [jnp.where(low, turned[j], turned[j + 1]) for j in range(0, NSEL, 2)], 1
            )
            grad = jnp.concatenate([g_v[q], jnp.zeros((heads, width - lat), BF16)], 1)
            both = jnp.concatenate([q_v[q], grad], 0)
            products.append(jnp.dot(both, kt, preferred_element_type=F32))
            keys.append(k)
        for i in range(STEP_ROWS):
            q = first + i
            scores = products[i][:heads] * score_scale
            d_prob = products[i][heads:]
            own = jnp.where(lane <= limit_ref[q], scores[:, :BLOCK], masked_score)
            scores = jnp.concatenate([own, scores[:, BLOCK:]], 1)
            e = jnp.exp(scores - jnp.max(scores, axis=1, keepdims=True))
            probs = e * (1.0 / jnp.sum(e, axis=1, keepdims=True))
            weights = probs.astype(BF16)
            delta = jnp.sum(weights.astype(F32) * d_prob, axis=1, keepdims=True)
            d_score = (probs * (d_prob - delta) * score_scale).astype(BF16)
            for j in range(NSEL):
                t = slice(j * BLOCK, (j + 1) * BLOCK)
                y_v[q * NSEL + j] = jnp.concatenate([d_score[:, t], weights[:, t]], 1)
            out = jnp.dot(
                jnp.concatenate([d_score, weights], 0), keys[i], preferred_element_type=F32
            )
            dq_v[buf, at * STEP_ROWS + i] = out[:heads].astype(BF16)
            o_v[buf, at * STEP_ROWS + i] = out[heads:, :lat].astype(BF16)
        return group

    def group(i, c):
        for x in in_copies(i):
            x.wait()

        @pl.when(i >= 2)
        def _():
            for x in out_copies(i - 2):
                x.wait()

        lax.fori_loop(0, COPY_ROWS // STEP_ROWS, step, i)
        for x in out_copies(i):
            x.start()
        return c

    lax.fori_loop(0, groups, group, 0)

    def key_step(place):
        names = [place * parts + h for h in range(parts)]
        counts = [cnt[s] for s in names]
        most = functools.reduce(jnp.maximum, counts)

        def chunk(c):
            sums = []
            for s, n in zip(names, counts):
                ys, qs, gs = [], [], []
                for i in range(CHUNK):
                    at = c * CHUNK + i
                    v = lst[s * rows + jnp.minimum(at, rows - 1)]
                    v = jnp.where(at < n, v, rows * 8)
                    q = v >> 3
                    ys.append(y_v[q * NSEL + (v & 7)])
                    q = jnp.minimum(q, rows - 1)
                    qs.append(q_v[q])
                    gs.append(g_v[q])
                y = jnp.concatenate(ys, 0).T
                a = jnp.dot(y[:BLOCK], jnp.concatenate(qs, 0), preferred_element_type=F32)
                b = jnp.dot(y[BLOCK:], jnp.concatenate(gs, 0), preferred_element_type=F32)
                sums.append(jnp.concatenate([a[:, :lat] + b, a[:, lat:]], 1))
            return sums

        for h, r in enumerate(chunk(0)):
            acc_v[h] = r

        def again(c, x):
            for h, r in enumerate(chunk(c)):
                acc_v[h] += r
            return x

        lax.fori_loop(1, (most + CHUNK - 1) // CHUNK, again, 0)

    def near_copies(place):
        b = lax.rem(place, 2)
        return [
            pltpu.make_async_copy(
                dk_v.at[b, :, pl.ds(c * piece, piece)], dk1_hbm.at[c, :, place], sem_dk.at[b, c]
            )
            for c in range(chunks)
        ]

    def far_copies_out(place):
        b = lax.rem(place, 2)
        return [pltpu.make_async_copy(dk_v.at[b], dk2_hbm.at[:, place - near], sem_dk.at[b, 0])]

    def key_loop(begin, end, copies):
        def body(place, c):
            key_step(place)

            @pl.when(place >= begin + 2)
            def _():
                for x in copies(place - 2):
                    x.wait()

            dk_v[lax.rem(place, 2)] = acc_v[...].astype(BF16)
            for x in copies(place):
                x.start()
            return c

        lax.fori_loop(begin, end, body, 0)
        for place in (end - 2, end - 1):
            for x in copies(jnp.int32(place)):
                x.wait()

    key_loop(0, near, near_copies)

    @pl.when(more)
    def _():
        key_loop(near, places, far_copies_out)

    for i in (groups - 2, groups - 1):
        for c in out_copies(jnp.int32(i)):
            c.wait()


def attend(count, slots, limit, queries, d_out, k1, k2):
    rows, heads, width = queries.shape
    lat = d_out.shape[2]
    parts, near = k1.shape[1:3]
    places = near + k2.shape[1]
    groups = rows // COPY_ROWS
    return pl.pallas_call(
        attend_kernel,
        out_shape=(
            jax.ShapeDtypeStruct((rows, heads, lat), BF16),
            jax.ShapeDtypeStruct((rows, heads, width), BF16),
            jax.ShapeDtypeStruct(k1.shape, BF16),
            jax.ShapeDtypeStruct(k2.shape, BF16),
        ),
        in_specs=[SMEM, SMEM, SMEM, HBM, HBM, HBM, HBM],
        out_specs=(HBM, HBM, HBM, HBM),
        scratch_shapes=[
            pltpu.VMEM((rows, heads, width), BF16),
            pltpu.VMEM((rows, heads, lat), BF16),
            pltpu.VMEM((parts, places, BLOCK, width), BF16),
            pltpu.VMEM((2, COPY_ROWS, heads, lat), BF16),
            pltpu.VMEM((2, COPY_ROWS, heads, width), BF16),
            pltpu.VMEM((2, parts, BLOCK, width), BF16),
            pltpu.VMEM((rows * NSEL + 1, heads, 2 * BLOCK), BF16),
            pltpu.VMEM((parts * places, width, 2 * BLOCK), BF16),
            pltpu.VMEM((parts, BLOCK, width), F32),
            pltpu.SMEM((parts * places,), jnp.int32),
            pltpu.SMEM((parts * places * rows,), jnp.int32),
            pltpu.SemaphoreType.DMA((groups, 2)),
            pltpu.SemaphoreType.DMA((CHUNKS + 1, parts)),
            pltpu.SemaphoreType.DMA((2, 2)),
            pltpu.SemaphoreType.DMA((2, CHUNKS)),
        ],
        compiler_params=pltpu.CompilerParams(vmem_limit_bytes=VMEM_BYTES),
        name="attend",
    )(count, slots, limit, queries, d_out, k1, k2)


def turn_kernel(src, out):
    out[...] = src[...].astype(F32).T


def widen_turned(rows):
    return pl.pallas_call(
        turn_kernel,
        out_shape=jax.ShapeDtypeStruct(rows.shape[::-1], F32),
        in_specs=[VMEM],
        out_specs=VMEM,
        compiler_params=pltpu.CompilerParams(vmem_limit_bytes=VMEM_BYTES),
        name="widen_turned",
    )(rows).T


def on_device(queries, cache, d_out, picks, q_pos):
    seq_count = lax.axis_size("seq")
    parts = lax.axis_size("head")
    part = lax.axis_index("head")
    rows, heads, width = queries.shape
    blocks_dev = cache.shape[0] // BLOCK
    all_blocks = seq_count * blocks_dev
    most_blocks = seq_count * 4
    places = most_blocks // parts
    near = -(-(POOL + rows // BLOCK) // parts)

    flat = picks.reshape(-1)
    block_ids = jnp.arange(all_blocks, dtype=jnp.int32)
    matches = flat[:, None] == block_ids[None, :]
    present = jnp.any(matches, axis=0)
    rank = jnp.cumsum(present.astype(jnp.int32)) - 1
    count = rank[-1] + 1
    slots = jnp.sum(jnp.where(matches, rank[None, :], 0), axis=1)
    mine = (present & (rank % parts == part)).reshape(seq_count, blocks_dev)
    wanted = jnp.max(
        jnp.where(mine, jnp.arange(blocks_dev, dtype=jnp.int32)[None, :], -1), axis=1
    )
    place_of = jnp.max(
        jnp.where(mine, rank.reshape(seq_count, blocks_dev) // parts, 0), axis=1
    )
    at_place = present[None, :] & (
        rank[None, :] == (jnp.arange(places, dtype=jnp.int32) * parts + part)[:, None]
    )
    owner_at = jnp.max(jnp.where(at_place, (block_ids // blocks_dev)[None, :], 0), axis=1)

    request = jnp.stack([wanted, jnp.full((seq_count,), count, jnp.int32)], axis=1)
    asked = lax.all_to_all(request, "seq", split_axis=0, concat_axis=0, tiled=True)
    blocks_asked = asked[:, 0]
    overflow = jnp.max(asked[:, 1]) > near * parts

    k1, fetched = fetch(
        jnp.maximum(blocks_asked, 0),
        owner_at[:near],
        cache.reshape(blocks_dev, BLOCK, width),
        near,
        parts,
    )
    far_shape = (parts, places - near, BLOCK, width)

    def gather_far(x):
        x = x.transpose(1, 0, 2, 3).reshape(seq_count, BLOCK, width)
        return lax.all_gather(take_blocks(owner_at[near:], x), "head", axis=0, tiled=False)

    k2 = lax.cond(overflow, gather_far, lambda x: unset(x, far_shape), fetched)
    out, d_queries, dk1, dk2 = attend(
        count[None], slots, q_pos % BLOCK, queries, d_out, k1, k2
    )
    r2 = lax.cond(
        overflow,
        lambda x: lax.psum_scatter(x, "head", scatter_dimension=0, tiled=False),
        lambda x: unset(x, far_shape[1:]),
        dk2,
    )
    returned = give_back(place_of, dk1, r2)
    owned = add_blocks(blocks_asked, returned, blocks_dev)
    d_cache = widen_turned(
        lax.psum_scatter(
            owned.reshape(blocks_dev * BLOCK, width), "head", scatter_dimension=0, tiled=True
        )
    )
    return (out, d_queries, d_cache)


def solution(mesh):
    placed = (
        P("seq", "head", None),
        P("seq", None),
        P("seq", "head", None),
        P("seq", None),
        P("seq"),
    )
    return jax.shard_map(
        on_device,
        mesh=mesh,
        in_specs=placed,
        out_specs=(P("seq", "head", None), P("seq", "head", None), P(("seq", "head"), None)),
        check_vma=False,
    )
```

```python
import functools
import math

import jax
import jax.numpy as jnp
from jax import lax
from jax.experimental import pallas as pl
from jax.experimental.pallas import tpu as pltpu
from jax.sharding import PartitionSpec as P

BLOCK = 64
POOL = 64
NSEL = 6

score_scale = 1.0 / math.sqrt(192.0)
masked_score = -1e30

BF16 = jnp.bfloat16
F32 = jnp.float32
COPY_ROWS = 16
STEP_ROWS = 16
CHUNK = 16
HBM = pl.BlockSpec(memory_space=pl.ANY)
SMEM = pl.BlockSpec(memory_space=pltpu.SMEM)
VMEM = pl.BlockSpec(memory_space=pltpu.VMEM)
VMEM_BYTES = 60 * 2**20
CHUNKS = 4
STRIDE = 13
MESH = pl.DeviceIdType.MESH


def take_blocks_kernel(index_ref, src, dst, sems):
    def copy(i):
        return pltpu.make_async_copy(src.at[index_ref[i]], dst.at[i], sems.at[i])

    def start(i, c):
        copy(i).start()
        return c

    def wait(i, c):
        copy(i).wait()
        return c

    lax.fori_loop(0, dst.shape[0], start, 0)
    lax.fori_loop(0, dst.shape[0], wait, 0)


def take_blocks(index, blocks):
    count = index.shape[0]
    return pl.pallas_call(
        take_blocks_kernel,
        out_shape=jax.ShapeDtypeStruct((count,) + blocks.shape[1:], blocks.dtype),
        in_specs=[SMEM, VMEM],
        out_specs=HBM,
        scratch_shapes=[pltpu.SemaphoreType.DMA((count,))],
        compiler_params=pltpu.CompilerParams(vmem_limit_bytes=VMEM_BYTES),
        name="take_blocks",
    )(index, blocks)


def unset_kernel(after_ref, out):
    del after_ref, out


def unset(after, shape):
    return pl.pallas_call(
        unset_kernel,
        out_shape=jax.ShapeDtypeStruct(shape, BF16),
        in_specs=[HBM],
        out_specs=HBM,
        name="unset",
    )(after)


def fetch_kernel(asked_ref, owner_ref, cache_v, near_hbm, all_hbm,
                 send_v, recv, pack_v, a_send, a_recv, x_send, x_recv, own_sem, all_sem):
    chunks, seq_count, rows, _ = send_v.shape
    near = pack_v.shape[1]
    parts = near_hbm.shape[1]
    cut = (near + 1) // 2
    me, part = lax.axis_index("seq"), lax.axis_index("head")
    right, left = lax.rem(part + 1, parts), lax.rem(part + parts - 1, parts)
    barrier = pltpu.get_barrier_semaphore()

    def greet(d, c):
        peer = lax.rem(me + d * STRIDE, seq_count)
        pl.semaphore_signal(barrier, inc=1, device_id=(peer, part), device_id_type=MESH)
        return c

    lax.fori_loop(1, seq_count, greet, 0)
    for x in (left, right):
        pl.semaphore_signal(barrier, inc=1, device_id=(me, x), device_id_type=MESH)
    for c in range(chunks):

        def serve(p, x, c=c):
            send_v[c, p] = cache_v[asked_ref[p], c * rows : (c + 1) * rows]
            return x

        lax.fori_loop(0, seq_count, serve, 0)
    pl.semaphore_wait(barrier, seq_count + 1)
    for c in range(chunks):

        def send(d, x, c=c):
            peer = lax.rem(me + d * STRIDE, seq_count)
            pltpu.make_async_remote_copy(
                src_ref=send_v.at[c, peer], dst_ref=recv[c].at[me],
                send_sem=a_send.at[c], recv_sem=a_recv.at[c],
                device_id=(peer, part), device_id_type=MESH,
            ).start()
            return x

        lax.fori_loop(1, seq_count, send, 0)
        recv[c][me] = send_v[c, me]

    def over_x(c, way, src, dst, to):
        return pltpu.make_async_remote_copy(
            src_ref=src, dst_ref=dst, send_sem=x_send.at[c, way], recv_sem=x_recv.at[c, way],
            device_id=(me, to), device_id_type=MESH,
        )

    def direct(c):
        out = near_hbm.at[c, part]
        return (over_x(c, 0, pack_v.at[c], out, right), over_x(c, 1, pack_v.at[c], out, left))

    def onward(c):
        one = near_hbm.at[c, left, pl.ds(0, cut)]
        two = near_hbm.at[c, right, pl.ds(cut, near - cut)]
        return (over_x(c, 2, one, one, right), over_x(c, 3, two, two, left))

    def own(c):
        return pltpu.make_async_copy(pack_v.at[c], near_hbm.at[c, part], own_sem.at[c])

    def keep(c):
        return pltpu.make_async_copy(recv[c], all_hbm.at[c], all_sem.at[c])

    def forward(c):
        for x, y in zip(direct(c), onward(c)):
            x.wait_recv()
            y.start()

    for c in range(chunks):
        whole = recv[c].at[pl.ds(0, seq_count - 1)]
        pltpu.make_async_copy(whole, whole, a_recv.at[c]).wait()

        def pack(i, x, c=c):
            pack_v[c, i] = recv[c][owner_ref[i]]
            return x

        lax.fori_loop(0, near, pack, 0)
        for x in direct(c):
            x.start()
        own(c).start()
        keep(c).start()
        if c:
            forward(c - 1)
    forward(chunks - 1)
    for c in range(chunks):
        whole = send_v.at[c, pl.ds(0, seq_count - 1)]
        pltpu.make_async_copy(whole, whole, a_send.at[c]).wait()
        own(c).wait()
        keep(c).wait()
        for x, y in zip(direct(c), onward(c)):
            x.wait_send()
            y.wait_send()
            y.wait_recv()


def fetch(asked, owner_at, blocks, near, parts):
    seq_count = asked.shape[0]
    width = blocks.shape[2]
    rows = BLOCK // CHUNKS
    dma = pltpu.SemaphoreType.DMA
    return pl.pallas_call(
        fetch_kernel,
        out_shape=(
            jax.ShapeDtypeStruct((CHUNKS, parts, near, rows, width), BF16),
            jax.ShapeDtypeStruct((CHUNKS, seq_count, rows, width), BF16),
        ),
        in_specs=[SMEM, SMEM, VMEM],
        out_specs=(HBM, HBM),
        scratch_shapes=[
            pltpu.VMEM((CHUNKS, seq_count, rows, width), BF16),
            [pltpu.VMEM((seq_count, rows, width), BF16)] * CHUNKS,
            pltpu.VMEM((CHUNKS, near, rows, width), BF16),
            dma((CHUNKS,)), dma((CHUNKS,)), dma((CHUNKS, 4)), dma((CHUNKS, 4)),
            dma((CHUNKS,)), dma((CHUNKS,)),
        ],
        compiler_params=pltpu.CompilerParams(
            vmem_limit_bytes=VMEM_BYTES, collective_id=1, has_side_effects=True
        ),
        name="fetch",
    )(asked, owner_at, blocks)


def give_back_kernel(place_ref, dk_hbm, far_v, out_hbm,
                     dk_v, sum_r, sum_l, one_l, one_r, two_l, two_r, places_v, back_v,
                     x_send, x_recv, a_send, a_recv, own_sem, load_sem):
    chunks, parts, near, rows, _ = dk_v.shape
    seq_count = back_v.shape[1]
    cut = (near + 1) // 2
    me, part = lax.axis_index("seq"), lax.axis_index("head")
    right, left = lax.rem(part + 1, parts), lax.rem(part + parts - 1, parts)
    far = lax.rem(part + 2, parts)
    barrier = pltpu.get_barrier_semaphore()

    def greet(d, c):
        peer = lax.rem(me + d * STRIDE, seq_count)
        pl.semaphore_signal(barrier, inc=1, device_id=(peer, part), device_id_type=MESH)
        return c

    lax.fori_loop(1, seq_count, greet, 0)
    for x in (left, right):
        pl.semaphore_signal(barrier, inc=1, device_id=(me, x), device_id_type=MESH)
    pl.semaphore_wait(barrier, seq_count + 1)

    def over_x(c, way, src, dst, to):
        return pltpu.make_async_remote_copy(
            src_ref=src, dst_ref=dst, send_sem=x_send.at[c, way], recv_sem=x_recv.at[c, way],
            device_id=(me, to), device_id_type=MESH,
        )

    def first(c):
        return (
            over_x(c, 0, dk_hbm.at[c, far, pl.ds(0, cut)], one_l.at[c], right),
            over_x(c, 1, dk_hbm.at[c, far, pl.ds(cut, near - cut)], one_r.at[c], left),
        )

    def second(c):
        return (
            over_x(c, 2, sum_r.at[c], two_l.at[c], right),
            over_x(c, 3, sum_l.at[c], two_r.at[c], left),
        )

    def own(c):
        return pltpu.make_async_copy(back_v.at[c, me], out_hbm.at[c, me], own_sem.at[c])

    def load(c):
        return pltpu.make_async_copy(dk_hbm.at[c], dk_v.at[c], load_sem.at[c])

    def begin(c):
        for x in first(c):
            x.start()

    def add_far(c):
        from_left, from_right = first(c)
        to_right, to_left = second(c)
        load(c).wait()
        from_left.wait_recv()
        sum_r[c, :cut] = (dk_v[c, right, :cut].astype(F32) + one_l[c].astype(F32)).astype(BF16)
        sum_r[c, cut:] = dk_v[c, right, cut:]
        to_right.start()
        from_right.wait_recv()
        sum_l[c, :cut] = dk_v[c, left, :cut]
        sum_l[c, cut:] = (dk_v[c, left, cut:].astype(F32) + one_r[c].astype(F32)).astype(BF16)
        to_left.start()

    def to_owners(c):
        for x in second(c):
            x.wait_recv()
        places_v[:near] = (
            dk_v[c, part].astype(F32) + two_l[c].astype(F32) + two_r[c].astype(F32)
        ).astype(BF16)
        places_v[near:] = far_v[:, c * rows : (c + 1) * rows]

        def place(o, x):
            back_v[c, o] = places_v[place_ref[o]]
            return x

        lax.fori_loop(0, seq_count, place, 0)

        def send(d, x):
            peer = lax.rem(me + d * STRIDE, seq_count)
            pltpu.make_async_remote_copy(
                src_ref=back_v.at[c, peer], dst_ref=out_hbm.at[c, me],
                send_sem=a_send.at[c], recv_sem=a_recv.at[c],
                device_id=(peer, part), device_id_type=MESH,
            ).start()
            return x

        lax.fori_loop(1, seq_count, send, 0)
        own(c).start()

    begin(0)
    begin(1)
    for c in range(chunks):
        load(c).start()
    for c in range(chunks + 1):
        if c < chunks:
            add_far(c)
        if c + 2 < chunks:
            begin(c + 2)
        if c:
            to_owners(c - 1)
    for c in range(chunks):
        whole = back_v.at[c, pl.ds(0, seq_count - 1)]
        pltpu.make_async_copy(whole, whole, a_send.at[c]).wait()
        landed = out_hbm.at[c, pl.ds(0, seq_count - 1)]
        pltpu.make_async_copy(landed, landed, a_recv.at[c]).wait()
        own(c).wait()
        for x in first(c) + second(c):
            x.wait_send()


def give_back(place_of, dk, far):
    chunks, parts, near, rows, width = dk.shape
    seq_count = place_of.shape[0]
    cut = (near + 1) // 2
    dma = pltpu.SemaphoreType.DMA
    piece = [pltpu.VMEM((chunks, n, rows, width), BF16)
             for n in (near, near, cut, near - cut, near, near)]
    return pl.pallas_call(
        give_back_kernel,
        out_shape=jax.ShapeDtypeStruct((chunks, seq_count, rows, width), BF16),
        in_specs=[SMEM, HBM, VMEM],
        out_specs=HBM,
        scratch_shapes=[pltpu.VMEM(dk.shape, BF16)] + piece + [
            pltpu.VMEM((near + far.shape[0], rows, width), BF16),
            pltpu.VMEM((chunks, seq_count, rows, width), BF16),
            dma((chunks, 4)), dma((chunks, 4)), dma((chunks,)), dma((chunks,)), dma((chunks,)),
            dma((chunks,)),
        ],
        compiler_params=pltpu.CompilerParams(
            vmem_limit_bytes=VMEM_BYTES, collective_id=2, has_side_effects=True
        ),
        name="give_back",
    )(place_of, dk, far)


def add_blocks_kernel(asked_ref, src, out, total):
    chunks, seq_count, rows, _ = src.shape
    total[...] = jnp.zeros_like(total)

    def add(i, x):
        block = asked_ref[i]

        @pl.when(block >= 0)
        def _():
            for c in range(chunks):
                total[block, c * rows : (c + 1) * rows] += src[c, i].astype(F32)

        return x

    lax.fori_loop(0, seq_count, add, 0)
    out[...] = total[...].astype(out.dtype)


def add_blocks(asked, returned, blocks_dev):
    shape = (blocks_dev, BLOCK, returned.shape[-1])
    return pl.pallas_call(
        add_blocks_kernel,
        out_shape=jax.ShapeDtypeStruct(shape, BF16),
        in_specs=[SMEM, VMEM],
        out_specs=VMEM,
        scratch_shapes=[pltpu.VMEM(shape, F32)],
        compiler_params=pltpu.CompilerParams(vmem_limit_bytes=VMEM_BYTES),
        name="add_blocks",
    )(asked, returned)


def attend_kernel(
    count_ref, slot_ref, limit_ref, q_hbm, g_hbm, k1_hbm, k2_hbm,
    o_hbm, dq_hbm, dk1_hbm, dk2_hbm,
    q_v, g_v, k_v, o_v, dq_v, dk_v, y_v, kt_v, acc_v, cnt, lst,
    sem_in, sem_k, sem_out, sem_dk,
):
    rows, heads, width = q_v.shape
    lat = g_v.shape[2]
    parts, places = k_v.shape[0], k_v.shape[1]
    chunks, _, near, piece, _ = k1_hbm.shape
    groups = rows // COPY_ROWS
    slots = parts * places
    more = count_ref[0] > parts * near

    def in_copies(i):
        s = pl.ds(i * COPY_ROWS, COPY_ROWS)
        return (
            pltpu.make_async_copy(q_hbm.at[s], q_v.at[s], sem_in.at[i, 0]),
            pltpu.make_async_copy(g_hbm.at[s], g_v.at[s], sem_in.at[i, 1]),
        )

    def out_copies(i):
        s = pl.ds(i * COPY_ROWS, COPY_ROWS)
        b = lax.rem(i, 2)
        return (
            pltpu.make_async_copy(o_v.at[b], o_hbm.at[s], sem_out.at[b, 0]),
            pltpu.make_async_copy(dq_v.at[b], dq_hbm.at[s], sem_out.at[b, 1]),
        )

    key_copies = [
        pltpu.make_async_copy(
            k1_hbm.at[c, h], k_v.at[h, pl.ds(0, near), pl.ds(c * piece, piece)], sem_k.at[c, h]
        )
        for c in range(chunks)
        for h in range(parts)
    ]
    far_copies = [
        pltpu.make_async_copy(
            k2_hbm.at[h], k_v.at[h, pl.ds(near, places - near)], sem_k.at[chunks, h]
        )
        for h in range(parts)
    ]
    for c in key_copies:
        c.start()

    @pl.when(more)
    def _():
        for c in far_copies:
            c.start()

    for i in range(groups):
        for c in in_copies(i):
            c.start()

    def clear(i, c):
        cnt[i] = 0
        return c

    lax.fori_loop(0, slots, clear, 0)
    y_v[rows * NSEL] = jnp.zeros((heads, 2 * BLOCK), BF16)
    for c in key_copies:
        c.wait()

    @pl.when(more)
    def _():
        for c in far_copies:
            c.wait()

    used = jnp.where(more, places, near)

    def turn(place, c):
        for h in range(parts):
            k = k_v[h, place]
            kt_v[place * parts + h] = jnp.concatenate([k, k], 0).T
        return c

    lax.fori_loop(0, used, turn, 0)

    lane = lax.broadcasted_iota(jnp.int32, (1, BLOCK), 1)
    low = lax.broadcasted_iota(jnp.int32, (width, 2 * BLOCK), 1) < BLOCK

    def step(at, group):
        first = group * COPY_ROWS + at * STEP_ROWS
        buf = lax.rem(group, 2)
        products, keys = [], []
        for i in range(STEP_ROWS):
            q = first + i
            picked, turned = [], []
            for j in range(NSEL):
                s = slot_ref[q * NSEL + j]
                c = cnt[s]
                lst[s * rows + c] = q * 8 + j
                cnt[s] = c + 1
                picked.append(k_v[s & 3, s >> 2])
                turned.append(kt_v[s])
            k = jnp.concatenate(picked, 0)
            kt = jnp.concatenate(
                [jnp.where(low, turned[j], turned[j + 1]) for j in range(0, NSEL, 2)], 1
            )
            grad = jnp.concatenate([g_v[q], jnp.zeros((heads, width - lat), BF16)], 1)
            both = jnp.concatenate([q_v[q], grad], 0)
            products.append(jnp.dot(both, kt, preferred_element_type=F32))
            keys.append(k)
        for i in range(STEP_ROWS):
            q = first + i
            scores = products[i][:heads] * score_scale
            d_prob = products[i][heads:]
            own = jnp.where(lane <= limit_ref[q], scores[:, :BLOCK], masked_score)
            scores = jnp.concatenate([own, scores[:, BLOCK:]], 1)
            e = jnp.exp(scores - jnp.max(scores, axis=1, keepdims=True))
            probs = e * (1.0 / jnp.sum(e, axis=1, keepdims=True))
            weights = probs.astype(BF16)
            delta = jnp.sum(weights.astype(F32) * d_prob, axis=1, keepdims=True)
            d_score = (probs * (d_prob - delta) * score_scale).astype(BF16)
            for j in range(NSEL):
                t = slice(j * BLOCK, (j + 1) * BLOCK)
                y_v[q * NSEL + j] = jnp.concatenate([d_score[:, t], weights[:, t]], 1)
            out = jnp.dot(
                jnp.concatenate([d_score, weights], 0), keys[i], preferred_element_type=F32
            )
            dq_v[buf, at * STEP_ROWS + i] = out[:heads].astype(BF16)
            o_v[buf, at * STEP_ROWS + i] = out[heads:, :lat].astype(BF16)
        return group

    def group(i, c):
        for x in in_copies(i):
            x.wait()

        @pl.when(i >= 2)
        def _():
            for x in out_copies(i - 2):
                x.wait()

        lax.fori_loop(0, COPY_ROWS // STEP_ROWS, step, i)
        for x in out_copies(i):
            x.start()
        return c

    lax.fori_loop(0, groups, group, 0)

    def key_step(place):
        names = [place * parts + h for h in range(parts)]
        counts = [cnt[s] for s in names]
        most = functools.reduce(jnp.maximum, counts)

        def chunk(c):
            sums = []
            for s, n in zip(names, counts):
                ys, qs, gs = [], [], []
                for i in range(CHUNK):
                    at = c * CHUNK + i
                    v = lst[s * rows + jnp.minimum(at, rows - 1)]
                    v = jnp.where(at < n, v, rows * 8)
                    q = v >> 3
                    ys.append(y_v[q * NSEL + (v & 7)])
                    q = jnp.minimum(q, rows - 1)
                    qs.append(q_v[q])
                    gs.append(g_v[q])
                y = jnp.concatenate(ys, 0).T
                a = jnp.dot(y[:BLOCK], jnp.concatenate(qs, 0), preferred_element_type=F32)
                b = jnp.dot(y[BLOCK:], jnp.concatenate(gs, 0), preferred_element_type=F32)
                sums.append(jnp.concatenate([a[:, :lat] + b, a[:, lat:]], 1))
            return sums

        for h, r in enumerate(chunk(0)):
            acc_v[h] = r

        def again(c, x):
            for h, r in enumerate(chunk(c)):
                acc_v[h] += r
            return x

        lax.fori_loop(1, (most + CHUNK - 1) // CHUNK, again, 0)

    def near_copies(place):
        b = lax.rem(place, 2)
        return [
            pltpu.make_async_copy(
                dk_v.at[b, :, pl.ds(c * piece, piece)], dk1_hbm.at[c, :, place], sem_dk.at[b, c]
            )
            for c in range(chunks)
        ]

    def far_copies_out(place):
        b = lax.rem(place, 2)
        return [pltpu.make_async_copy(dk_v.at[b], dk2_hbm.at[:, place - near], sem_dk.at[b, 0])]

    def key_loop(begin, end, copies):
        def body(place, c):
            key_step(place)

            @pl.when(place >= begin + 2)
            def _():
                for x in copies(place - 2):
                    x.wait()

            dk_v[lax.rem(place, 2)] = acc_v[...].astype(BF16)
            for x in copies(place):
                x.start()
            return c

        lax.fori_loop(begin, end, body, 0)
        for place in (end - 2, end - 1):
            for x in copies(jnp.int32(place)):
                x.wait()

    key_loop(0, near, near_copies)

    @pl.when(more)
    def _():
        key_loop(near, places, far_copies_out)

    for i in (groups - 2, groups - 1):
        for c in out_copies(jnp.int32(i)):
            c.wait()


def attend(count, slots, limit, queries, d_out, k1, k2):
    rows, heads, width = queries.shape
    lat = d_out.shape[2]
    parts, near = k1.shape[1:3]
    places = near + k2.shape[1]
    groups = rows // COPY_ROWS
    return pl.pallas_call(
        attend_kernel,
        out_shape=(
            jax.ShapeDtypeStruct((rows, heads, lat), BF16),
            jax.ShapeDtypeStruct((rows, heads, width), BF16),
            jax.ShapeDtypeStruct(k1.shape, BF16),
            jax.ShapeDtypeStruct(k2.shape, BF16),
        ),
        in_specs=[SMEM, SMEM, SMEM, HBM, HBM, HBM, HBM],
        out_specs=(HBM, HBM, HBM, HBM),
        scratch_shapes=[
            pltpu.VMEM((rows, heads, width), BF16),
            pltpu.VMEM((rows, heads, lat), BF16),
            pltpu.VMEM((parts, places, BLOCK, width), BF16),
            pltpu.VMEM((2, COPY_ROWS, heads, lat), BF16),
            pltpu.VMEM((2, COPY_ROWS, heads, width), BF16),
            pltpu.VMEM((2, parts, BLOCK, width), BF16),
            pltpu.VMEM((rows * NSEL + 1, heads, 2 * BLOCK), BF16),
            pltpu.VMEM((parts * places, width, 2 * BLOCK), BF16),
            pltpu.VMEM((parts, BLOCK, width), F32),
            pltpu.SMEM((parts * places,), jnp.int32),
            pltpu.SMEM((parts * places * rows,), jnp.int32),
            pltpu.SemaphoreType.DMA((groups, 2)),
            pltpu.SemaphoreType.DMA((CHUNKS + 1, parts)),
            pltpu.SemaphoreType.DMA((2, 2)),
            pltpu.SemaphoreType.DMA((2, CHUNKS)),
        ],
        compiler_params=pltpu.CompilerParams(vmem_limit_bytes=VMEM_BYTES),
        name="attend",
    )(count, slots, limit, queries, d_out, k1, k2)


def turn_kernel(src, out):
    out[...] = src[...].astype(F32).T


def widen_turned(rows):
    return pl.pallas_call(
        turn_kernel,
        out_shape=jax.ShapeDtypeStruct(rows.shape[::-1], F32),
        in_specs=[VMEM],
        out_specs=VMEM,
        compiler_params=pltpu.CompilerParams(vmem_limit_bytes=VMEM_BYTES),
        name="widen_turned",
    )(rows).T


def on_device(queries, cache, d_out, picks, q_pos):
    seq_count = lax.axis_size("seq")
    parts = lax.axis_size("head")
    part = lax.axis_index("head")
    rows, heads, width = queries.shape
    blocks_dev = cache.shape[0] // BLOCK
    all_blocks = seq_count * blocks_dev
    most_blocks = seq_count * 4
    places = most_blocks // parts
    near = -(-(POOL + rows // BLOCK) // parts)

    flat = picks.reshape(-1)
    block_ids = jnp.arange(all_blocks, dtype=jnp.int32)
    matches = flat[:, None] == block_ids[None, :]
    present = jnp.any(matches, axis=0)
    rank = jnp.cumsum(present.astype(jnp.int32)) - 1
    count = rank[-1] + 1
    slots = jnp.sum(jnp.where(matches, rank[None, :], 0), axis=1)
    mine = (present & (rank % parts == part)).reshape(seq_count, blocks_dev)
    wanted = jnp.max(
        jnp.where(mine, jnp.arange(blocks_dev, dtype=jnp.int32)[None, :], -1), axis=1
    )
    place_of = jnp.max(
        jnp.where(mine, rank.reshape(seq_count, blocks_dev) // parts, 0), axis=1
    )
    at_place = present[None, :] & (
        rank[None, :] == (jnp.arange(places, dtype=jnp.int32) * parts + part)[:, None]
    )
    owner_at = jnp.max(jnp.where(at_place, (block_ids // blocks_dev)[None, :], 0), axis=1)

    request = jnp.stack([wanted, jnp.full((seq_count,), count, jnp.int32)], axis=1)
    asked = lax.all_to_all(request, "seq", split_axis=0, concat_axis=0, tiled=True)
    blocks_asked = asked[:, 0]
    overflow = jnp.max(asked[:, 1]) > near * parts

    k1, fetched = fetch(
        jnp.maximum(blocks_asked, 0),
        owner_at[:near],
        cache.reshape(blocks_dev, BLOCK, width),
        near,
        parts,
    )
    far_shape = (parts, places - near, BLOCK, width)

    def gather_far(x):
        x = x.transpose(1, 0, 2, 3).reshape(seq_count, BLOCK, width)
        return lax.all_gather(take_blocks(owner_at[near:], x), "head", axis=0, tiled=False)

    k2 = lax.cond(overflow, gather_far, lambda x: unset(x, far_shape), fetched)
    out, d_queries, dk1, dk2 = attend(
        count[None], slots, q_pos % BLOCK, queries, d_out, k1, k2
    )
    r2 = lax.cond(
        overflow,
        lambda x: lax.psum_scatter(x, "head", scatter_dimension=0, tiled=False),
        lambda x: unset(x, far_shape[1:]),
        dk2,
    )
    returned = give_back(place_of, dk1, r2)
    owned = add_blocks(blocks_asked, returned, blocks_dev)
    d_cache = widen_turned(
        lax.psum_scatter(
            owned.reshape(blocks_dev * BLOCK, width), "head", scatter_dimension=0, tiled=True
        )
    )
    return (out, d_queries, d_cache)


def solution(mesh):
    placed = (
        P("seq", "head", None),
        P("seq", None),
        P("seq", "head", None),
        P("seq", None),
        P("seq"),
    )
    return jax.shard_map(
        on_device,
        mesh=mesh,
        in_specs=placed,
        out_specs=(P("seq", "head", None), P("seq", "head", None), P(("seq", "head"), None)),
        check_vma=False,
    )
```

```python
import functools
import math

import jax
import jax.numpy as jnp
from jax import lax
from jax.experimental import pallas as pl
from jax.experimental.pallas import tpu as pltpu
from jax.sharding import PartitionSpec as P

BLOCK = 64
POOL = 64
NSEL = 6

score_scale = 1.0 / math.sqrt(192.0)
masked_score = -1e30

BF16 = jnp.bfloat16
F32 = jnp.float32
COPY_ROWS = 16
STEP_ROWS = 16
CHUNK = 8
HBM = pl.BlockSpec(memory_space=pl.ANY)
SMEM = pl.BlockSpec(memory_space=pltpu.SMEM)
VMEM = pl.BlockSpec(memory_space=pltpu.VMEM)
VMEM_BYTES = 60 * 2**20
CHUNKS = 4
STRIDE = 13
MESH = pl.DeviceIdType.MESH


def take_blocks_kernel(index_ref, src, dst, sems):
    def copy(i):
        return pltpu.make_async_copy(src.at[index_ref[i]], dst.at[i], sems.at[i])

    def start(i, c):
        copy(i).start()
        return c

    def wait(i, c):
        copy(i).wait()
        return c

    lax.fori_loop(0, dst.shape[0], start, 0)
    lax.fori_loop(0, dst.shape[0], wait, 0)


def take_blocks(index, blocks):
    count = index.shape[0]
    return pl.pallas_call(
        take_blocks_kernel,
        out_shape=jax.ShapeDtypeStruct((count,) + blocks.shape[1:], blocks.dtype),
        in_specs=[SMEM, VMEM],
        out_specs=HBM,
        scratch_shapes=[pltpu.SemaphoreType.DMA((count,))],
        compiler_params=pltpu.CompilerParams(vmem_limit_bytes=VMEM_BYTES),
        name="take_blocks",
    )(index, blocks)


def unset_kernel(after_ref, out):
    del after_ref, out


def unset(after, shape):
    return pl.pallas_call(
        unset_kernel,
        out_shape=jax.ShapeDtypeStruct(shape, BF16),
        in_specs=[HBM],
        out_specs=HBM,
        name="unset",
    )(after)


def fetch_kernel(asked_ref, owner_ref, cache_v, near_hbm, all_hbm,
                 send_v, recv, pack_v, a_send, a_recv, x_send, x_recv, own_sem, all_sem):
    chunks, seq_count, rows, _ = send_v.shape
    near = pack_v.shape[1]
    parts = near_hbm.shape[1]
    cut = (near + 1) // 2
    me, part = lax.axis_index("seq"), lax.axis_index("head")
    right, left = lax.rem(part + 1, parts), lax.rem(part + parts - 1, parts)
    barrier = pltpu.get_barrier_semaphore()

    def greet(d, c):
        peer = lax.rem(me + d * STRIDE, seq_count)
        pl.semaphore_signal(barrier, inc=1, device_id=(peer, part), device_id_type=MESH)
        return c

    lax.fori_loop(1, seq_count, greet, 0)
    for x in (left, right):
        pl.semaphore_signal(barrier, inc=1, device_id=(me, x), device_id_type=MESH)
    for c in range(chunks):

        def serve(p, x, c=c):
            send_v[c, p] = cache_v[asked_ref[p], c * rows : (c + 1) * rows]
            return x

        lax.fori_loop(0, seq_count, serve, 0)
    pl.semaphore_wait(barrier, seq_count + 1)
    for c in range(chunks):

        def send(d, x, c=c):
            peer = lax.rem(me + d * STRIDE, seq_count)
            pltpu.make_async_remote_copy(
                src_ref=send_v.at[c, peer], dst_ref=recv[c].at[me],
                send_sem=a_send.at[c], recv_sem=a_recv.at[c],
                device_id=(peer, part), device_id_type=MESH,
            ).start()
            return x

        lax.fori_loop(1, seq_count, send, 0)
        recv[c][me] = send_v[c, me]

    def over_x(c, way, src, dst, to):
        return pltpu.make_async_remote_copy(
            src_ref=src, dst_ref=dst, send_sem=x_send.at[c, way], recv_sem=x_recv.at[c, way],
            device_id=(me, to), device_id_type=MESH,
        )

    def direct(c):
        out = near_hbm.at[c, part]
        return (over_x(c, 0, pack_v.at[c], out, right), over_x(c, 1, pack_v.at[c], out, left))

    def onward(c):
        one = near_hbm.at[c, left, pl.ds(0, cut)]
        two = near_hbm.at[c, right, pl.ds(cut, near - cut)]
        return (over_x(c, 2, one, one, right), over_x(c, 3, two, two, left))

    def own(c):
        return pltpu.make_async_copy(pack_v.at[c], near_hbm.at[c, part], own_sem.at[c])

    def keep(c):
        return pltpu.make_async_copy(recv[c], all_hbm.at[c], all_sem.at[c])

    def forward(c):
        for x, y in zip(direct(c), onward(c)):
            x.wait_recv()
            y.start()

    for c in range(chunks):
        whole = recv[c].at[pl.ds(0, seq_count - 1)]
        pltpu.make_async_copy(whole, whole, a_recv.at[c]).wait()

        def pack(i, x, c=c):
            pack_v[c, i] = recv[c][owner_ref[i]]
            return x

        lax.fori_loop(0, near, pack, 0)
        for x in direct(c):
            x.start()
        own(c).start()
        keep(c).start()
        if c:
            forward(c - 1)
    forward(chunks - 1)
    for c in range(chunks):
        whole = send_v.at[c, pl.ds(0, seq_count - 1)]
        pltpu.make_async_copy(whole, whole, a_send.at[c]).wait()
        own(c).wait()
        keep(c).wait()
        for x, y in zip(direct(c), onward(c)):
            x.wait_send()
            y.wait_send()
            y.wait_recv()


def fetch(asked, owner_at, blocks, near, parts):
    seq_count = asked.shape[0]
    width = blocks.shape[2]
    rows = BLOCK // CHUNKS
    dma = pltpu.SemaphoreType.DMA
    return pl.pallas_call(
        fetch_kernel,
        out_shape=(
            jax.ShapeDtypeStruct((CHUNKS, parts, near, rows, width), BF16),
            jax.ShapeDtypeStruct((CHUNKS, seq_count, rows, width), BF16),
        ),
        in_specs=[SMEM, SMEM, VMEM],
        out_specs=(HBM, HBM),
        scratch_shapes=[
            pltpu.VMEM((CHUNKS, seq_count, rows, width), BF16),
            [pltpu.VMEM((seq_count, rows, width), BF16)] * CHUNKS,
            pltpu.VMEM((CHUNKS, near, rows, width), BF16),
            dma((CHUNKS,)), dma((CHUNKS,)), dma((CHUNKS, 4)), dma((CHUNKS, 4)),
            dma((CHUNKS,)), dma((CHUNKS,)),
        ],
        compiler_params=pltpu.CompilerParams(
            vmem_limit_bytes=VMEM_BYTES, collective_id=1, has_side_effects=True
        ),
        name="fetch",
    )(asked, owner_at, blocks)


def give_back_kernel(place_ref, dk_hbm, far_v, out_hbm,
                     dk_v, sum_r, sum_l, one_l, one_r, two_l, two_r, places_v, back_v,
                     x_send, x_recv, a_send, a_recv, own_sem, load_sem):
    chunks, parts, near, rows, _ = dk_v.shape
    seq_count = back_v.shape[1]
    cut = (near + 1) // 2
    me, part = lax.axis_index("seq"), lax.axis_index("head")
    right, left = lax.rem(part + 1, parts), lax.rem(part + parts - 1, parts)
    far = lax.rem(part + 2, parts)
    barrier = pltpu.get_barrier_semaphore()

    def greet(d, c):
        peer = lax.rem(me + d * STRIDE, seq_count)
        pl.semaphore_signal(barrier, inc=1, device_id=(peer, part), device_id_type=MESH)
        return c

    lax.fori_loop(1, seq_count, greet, 0)
    for x in (left, right):
        pl.semaphore_signal(barrier, inc=1, device_id=(me, x), device_id_type=MESH)
    pl.semaphore_wait(barrier, seq_count + 1)

    def over_x(c, way, src, dst, to):
        return pltpu.make_async_remote_copy(
            src_ref=src, dst_ref=dst, send_sem=x_send.at[c, way], recv_sem=x_recv.at[c, way],
            device_id=(me, to), device_id_type=MESH,
        )

    def first(c):
        return (
            over_x(c, 0, dk_hbm.at[c, far, pl.ds(0, cut)], one_l.at[c], right),
            over_x(c, 1, dk_hbm.at[c, far, pl.ds(cut, near - cut)], one_r.at[c], left),
        )

    def second(c):
        return (
            over_x(c, 2, sum_r.at[c], two_l.at[c], right),
            over_x(c, 3, sum_l.at[c], two_r.at[c], left),
        )

    def own(c):
        return pltpu.make_async_copy(back_v.at[c, me], out_hbm.at[c, me], own_sem.at[c])

    def load(c):
        return pltpu.make_async_copy(dk_hbm.at[c], dk_v.at[c], load_sem.at[c])

    def begin(c):
        for x in first(c):
            x.start()

    def add_far(c):
        from_left, from_right = first(c)
        to_right, to_left = second(c)
        load(c).wait()
        from_left.wait_recv()
        sum_r[c, :cut] = (dk_v[c, right, :cut].astype(F32) + one_l[c].astype(F32)).astype(BF16)
        sum_r[c, cut:] = dk_v[c, right, cut:]
        to_right.start()
        from_right.wait_recv()
        sum_l[c, :cut] = dk_v[c, left, :cut]
        sum_l[c, cut:] = (dk_v[c, left, cut:].astype(F32) + one_r[c].astype(F32)).astype(BF16)
        to_left.start()

    def to_owners(c):
        for x in second(c):
            x.wait_recv()
        places_v[:near] = (
            dk_v[c, part].astype(F32) + two_l[c].astype(F32) + two_r[c].astype(F32)
        ).astype(BF16)
        places_v[near:] = far_v[:, c * rows : (c + 1) * rows]

        def place(o, x):
            back_v[c, o] = places_v[place_ref[o]]
            return x

        lax.fori_loop(0, seq_count, place, 0)

        def send(d, x):
            peer = lax.rem(me + d * STRIDE, seq_count)
            pltpu.make_async_remote_copy(
                src_ref=back_v.at[c, peer], dst_ref=out_hbm.at[c, me],
                send_sem=a_send.at[c], recv_sem=a_recv.at[c],
                device_id=(peer, part), device_id_type=MESH,
            ).start()
            return x

        lax.fori_loop(1, seq_count, send, 0)
        own(c).start()

    begin(0)
    begin(1)
    for c in range(chunks):
        load(c).start()
    for c in range(chunks + 1):
        if c < chunks:
            add_far(c)
        if c + 2 < chunks:
            begin(c + 2)
        if c:
            to_owners(c - 1)
    for c in range(chunks):
        whole = back_v.at[c, pl.ds(0, seq_count - 1)]
        pltpu.make_async_copy(whole, whole, a_send.at[c]).wait()
        landed = out_hbm.at[c, pl.ds(0, seq_count - 1)]
        pltpu.make_async_copy(landed, landed, a_recv.at[c]).wait()
        own(c).wait()
        for x in first(c) + second(c):
            x.wait_send()


def give_back(place_of, dk, far):
    chunks, parts, near, rows, width = dk.shape
    seq_count = place_of.shape[0]
    cut = (near + 1) // 2
    dma = pltpu.SemaphoreType.DMA
    piece = [pltpu.VMEM((chunks, n, rows, width), BF16)
             for n in (near, near, cut, near - cut, near, near)]
    return pl.pallas_call(
        give_back_kernel,
        out_shape=jax.ShapeDtypeStruct((chunks, seq_count, rows, width), BF16),
        in_specs=[SMEM, HBM, VMEM],
        out_specs=HBM,
        scratch_shapes=[pltpu.VMEM(dk.shape, BF16)] + piece + [
            pltpu.VMEM((near + far.shape[0], rows, width), BF16),
            pltpu.VMEM((chunks, seq_count, rows, width), BF16),
            dma((chunks, 4)), dma((chunks, 4)), dma((chunks,)), dma((chunks,)), dma((chunks,)),
            dma((chunks,)),
        ],
        compiler_params=pltpu.CompilerParams(
            vmem_limit_bytes=VMEM_BYTES, collective_id=2, has_side_effects=True
        ),
        name="give_back",
    )(place_of, dk, far)


def add_blocks_kernel(asked_ref, src, out, total):
    chunks, seq_count, rows, _ = src.shape
    total[...] = jnp.zeros_like(total)

    def add(i, x):
        block = asked_ref[i]

        @pl.when(block >= 0)
        def _():
            for c in range(chunks):
                total[block, c * rows : (c + 1) * rows] += src[c, i].astype(F32)

        return x

    lax.fori_loop(0, seq_count, add, 0)
    out[...] = total[...].astype(out.dtype)


def add_blocks(asked, returned, blocks_dev):
    shape = (blocks_dev, BLOCK, returned.shape[-1])
    return pl.pallas_call(
        add_blocks_kernel,
        out_shape=jax.ShapeDtypeStruct(shape, BF16),
        in_specs=[SMEM, VMEM],
        out_specs=VMEM,
        scratch_shapes=[pltpu.VMEM(shape, F32)],
        compiler_params=pltpu.CompilerParams(vmem_limit_bytes=VMEM_BYTES),
        name="add_blocks",
    )(asked, returned)


def attend_kernel(
    count_ref, slot_ref, limit_ref, q_hbm, g_hbm, k1_hbm, k2_hbm,
    o_hbm, dq_hbm, dk1_hbm, dk2_hbm,
    q_v, g_v, k_v, o_v, dq_v, dk_v, y_v, kt_v, acc_v, cnt, lst,
    sem_in, sem_k, sem_out, sem_dk,
):
    rows, heads, width = q_v.shape
    lat = g_v.shape[2]
    parts, places = k_v.shape[0], k_v.shape[1]
    chunks, _, near, piece, _ = k1_hbm.shape
    groups = rows // COPY_ROWS
    slots = parts * places
    more = count_ref[0] > parts * near

    def in_copies(i):
        s = pl.ds(i * COPY_ROWS, COPY_ROWS)
        return (
            pltpu.make_async_copy(q_hbm.at[s], q_v.at[s], sem_in.at[i, 0]),
            pltpu.make_async_copy(g_hbm.at[s], g_v.at[s], sem_in.at[i, 1]),
        )

    def out_copies(i):
        s = pl.ds(i * COPY_ROWS, COPY_ROWS)
        b = lax.rem(i, 2)
        return (
            pltpu.make_async_copy(o_v.at[b], o_hbm.at[s], sem_out.at[b, 0]),
            pltpu.make_async_copy(dq_v.at[b], dq_hbm.at[s], sem_out.at[b, 1]),
        )

    key_copies = [
        pltpu.make_async_copy(
            k1_hbm.at[c, h], k_v.at[h, pl.ds(0, near), pl.ds(c * piece, piece)], sem_k.at[c, h]
        )
        for c in range(chunks)
        for h in range(parts)
    ]
    far_copies = [
        pltpu.make_async_copy(
            k2_hbm.at[h], k_v.at[h, pl.ds(near, places - near)], sem_k.at[chunks, h]
        )
        for h in range(parts)
    ]
    for c in key_copies:
        c.start()

    @pl.when(more)
    def _():
        for c in far_copies:
            c.start()

    for i in range(groups):
        for c in in_copies(i):
            c.start()

    def clear(i, c):
        cnt[i] = 0
        return c

    lax.fori_loop(0, slots, clear, 0)
    y_v[rows * NSEL] = jnp.zeros((heads, 2 * BLOCK), BF16)
    for c in key_copies:
        c.wait()

    @pl.when(more)
    def _():
        for c in far_copies:
            c.wait()

    used = jnp.where(more, places, near)

    def turn(place, c):
        for h in range(parts):
            k = k_v[h, place]
            kt_v[place * parts + h] = jnp.concatenate([k, k], 0).T
        return c

    lax.fori_loop(0, used, turn, 0)

    lane = lax.broadcasted_iota(jnp.int32, (1, BLOCK), 1)
    low = lax.broadcasted_iota(jnp.int32, (width, 2 * BLOCK), 1) < BLOCK

    def step(at, group):
        first = group * COPY_ROWS + at * STEP_ROWS
        buf = lax.rem(group, 2)
        products, keys = [], []
        for i in range(STEP_ROWS):
            q = first + i
            picked, turned = [], []
            for j in range(NSEL):
                s = slot_ref[q * NSEL + j]
                c = cnt[s]
                lst[s * rows + c] = q * 8 + j
                cnt[s] = c + 1
                picked.append(k_v[s & 3, s >> 2])
                turned.append(kt_v[s])
            k = jnp.concatenate(picked, 0)
            kt = jnp.concatenate(
                [jnp.where(low, turned[j], turned[j + 1]) for j in range(0, NSEL, 2)], 1
            )
            grad = jnp.concatenate([g_v[q], jnp.zeros((heads, width - lat), BF16)], 1)
            both = jnp.concatenate([q_v[q], grad], 0)
            products.append(jnp.dot(both, kt, preferred_element_type=F32))
            keys.append(k)
        for i in range(STEP_ROWS):
            q = first + i
            scores = products[i][:heads] * score_scale
            d_prob = products[i][heads:]
            own = jnp.where(lane <= limit_ref[q], scores[:, :BLOCK], masked_score)
            scores = jnp.concatenate([own, scores[:, BLOCK:]], 1)
            e = jnp.exp(scores - jnp.max(scores, axis=1, keepdims=True))
            probs = e * (1.0 / jnp.sum(e, axis=1, keepdims=True))
            weights = probs.astype(BF16)
            delta = jnp.sum(weights.astype(F32) * d_prob, axis=1, keepdims=True)
            d_score = (probs * (d_prob - delta) * score_scale).astype(BF16)
            for j in range(NSEL):
                t = slice(j * BLOCK, (j + 1) * BLOCK)
                y_v[q * NSEL + j] = jnp.concatenate([d_score[:, t], weights[:, t]], 1)
            out = jnp.dot(
                jnp.concatenate([d_score, weights], 0), keys[i], preferred_element_type=F32
            )
            dq_v[buf, at * STEP_ROWS + i] = out[:heads].astype(BF16)
            o_v[buf, at * STEP_ROWS + i] = out[heads:, :lat].astype(BF16)
        return group

    def group(i, c):
        for x in in_copies(i):
            x.wait()

        @pl.when(i >= 2)
        def _():
            for x in out_copies(i - 2):
                x.wait()

        lax.fori_loop(0, COPY_ROWS // STEP_ROWS, step, i)
        for x in out_copies(i):
            x.start()
        return c

    lax.fori_loop(0, groups, group, 0)

    def key_step(place):
        names = [place * parts + h for h in range(parts)]
        counts = [cnt[s] for s in names]
        most = functools.reduce(jnp.maximum, counts)

        def chunk(c):
            sums = []
            for s, n in zip(names, counts):
                ys, qs, gs = [], [], []
                for i in range(CHUNK):
                    at = c * CHUNK + i
                    v = lst[s * rows + jnp.minimum(at, rows - 1)]
                    v = jnp.where(at < n, v, rows * 8)
                    q = v >> 3
                    ys.append(y_v[q * NSEL + (v & 7)])
                    q = jnp.minimum(q, rows - 1)
                    qs.append(q_v[q])
                    gs.append(g_v[q])
                y = jnp.concatenate(ys, 0).T
                a = jnp.dot(y[:BLOCK], jnp.concatenate(qs, 0), preferred_element_type=F32)
                b = jnp.dot(y[BLOCK:], jnp.concatenate(gs, 0), preferred_element_type=F32)
                sums.append(jnp.concatenate([a[:, :lat] + b, a[:, lat:]], 1))
            return sums

        for h, r in enumerate(chunk(0)):
            acc_v[h] = r

        def again(c, x):
            for h, r in enumerate(chunk(c)):
                acc_v[h] += r
            return x

        lax.fori_loop(1, (most + CHUNK - 1) // CHUNK, again, 0)

    def near_copies(place):
        b = lax.rem(place, 2)
        return [
            pltpu.make_async_copy(
                dk_v.at[b, :, pl.ds(c * piece, piece)], dk1_hbm.at[c, :, place], sem_dk.at[b, c]
            )
            for c in range(chunks)
        ]

    def far_copies_out(place):
        b = lax.rem(place, 2)
        return [pltpu.make_async_copy(dk_v.at[b], dk2_hbm.at[:, place - near], sem_dk.at[b, 0])]

    def key_loop(begin, end, copies):
        def body(place, c):
            key_step(place)

            @pl.when(place >= begin + 2)
            def _():
                for x in copies(place - 2):
                    x.wait()

            dk_v[lax.rem(place, 2)] = acc_v[...].astype(BF16)
            for x in copies(place):
                x.start()
            return c

        lax.fori_loop(begin, end, body, 0)
        for place in (end - 2, end - 1):
            for x in copies(jnp.int32(place)):
                x.wait()

    key_loop(0, near, near_copies)

    @pl.when(more)
    def _():
        key_loop(near, places, far_copies_out)

    for i in (groups - 2, groups - 1):
        for c in out_copies(jnp.int32(i)):
            c.wait()


def attend(count, slots, limit, queries, d_out, k1, k2):
    rows, heads, width = queries.shape
    lat = d_out.shape[2]
    parts, near = k1.shape[1:3]
    places = near + k2.shape[1]
    groups = rows // COPY_ROWS
    return pl.pallas_call(
        attend_kernel,
        out_shape=(
            jax.ShapeDtypeStruct((rows, heads, lat), BF16),
            jax.ShapeDtypeStruct((rows, heads, width), BF16),
            jax.ShapeDtypeStruct(k1.shape, BF16),
            jax.ShapeDtypeStruct(k2.shape, BF16),
        ),
        in_specs=[SMEM, SMEM, SMEM, HBM, HBM, HBM, HBM],
        out_specs=(HBM, HBM, HBM, HBM),
        scratch_shapes=[
            pltpu.VMEM((rows, heads, width), BF16),
            pltpu.VMEM((rows, heads, lat), BF16),
            pltpu.VMEM((parts, places, BLOCK, width), BF16),
            pltpu.VMEM((2, COPY_ROWS, heads, lat), BF16),
            pltpu.VMEM((2, COPY_ROWS, heads, width), BF16),
            pltpu.VMEM((2, parts, BLOCK, width), BF16),
            pltpu.VMEM((rows * NSEL + 1, heads, 2 * BLOCK), BF16),
            pltpu.VMEM((parts * places, width, 2 * BLOCK), BF16),
            pltpu.VMEM((parts, BLOCK, width), F32),
            pltpu.SMEM((parts * places,), jnp.int32),
            pltpu.SMEM((parts * places * rows,), jnp.int32),
            pltpu.SemaphoreType.DMA((groups, 2)),
            pltpu.SemaphoreType.DMA((CHUNKS + 1, parts)),
            pltpu.SemaphoreType.DMA((2, 2)),
            pltpu.SemaphoreType.DMA((2, CHUNKS)),
        ],
        compiler_params=pltpu.CompilerParams(vmem_limit_bytes=VMEM_BYTES),
        name="attend",
    )(count, slots, limit, queries, d_out, k1, k2)


def turn_kernel(src, out):
    out[...] = src[...].astype(F32).T


def widen_turned(rows):
    return pl.pallas_call(
        turn_kernel,
        out_shape=jax.ShapeDtypeStruct(rows.shape[::-1], F32),
        in_specs=[VMEM],
        out_specs=VMEM,
        compiler_params=pltpu.CompilerParams(vmem_limit_bytes=VMEM_BYTES),
        name="widen_turned",
    )(rows).T


def on_device(queries, cache, d_out, picks, q_pos):
    seq_count = lax.axis_size("seq")
    parts = lax.axis_size("head")
    part = lax.axis_index("head")
    rows, heads, width = queries.shape
    blocks_dev = cache.shape[0] // BLOCK
    all_blocks = seq_count * blocks_dev
    most_blocks = seq_count * 4
    places = most_blocks // parts
    near = -(-(POOL + rows // BLOCK) // parts)

    flat = picks.reshape(-1)
    block_ids = jnp.arange(all_blocks, dtype=jnp.int32)
    matches = flat[:, None] == block_ids[None, :]
    present = jnp.any(matches, axis=0)
    rank = jnp.cumsum(present.astype(jnp.int32)) - 1
    count = rank[-1] + 1
    slots = jnp.sum(jnp.where(matches, rank[None, :], 0), axis=1)
    mine = (present & (rank % parts == part)).reshape(seq_count, blocks_dev)
    wanted = jnp.max(
        jnp.where(mine, jnp.arange(blocks_dev, dtype=jnp.int32)[None, :], -1), axis=1
    )
    place_of = jnp.max(
        jnp.where(mine, rank.reshape(seq_count, blocks_dev) // parts, 0), axis=1
    )
    at_place = present[None, :] & (
        rank[None, :] == (jnp.arange(places, dtype=jnp.int32) * parts + part)[:, None]
    )
    owner_at = jnp.max(jnp.where(at_place, (block_ids // blocks_dev)[None, :], 0), axis=1)

    request = jnp.stack([wanted, jnp.full((seq_count,), count, jnp.int32)], axis=1)
    asked = lax.all_to_all(request, "seq", split_axis=0, concat_axis=0, tiled=True)
    blocks_asked = asked[:, 0]
    overflow = jnp.max(asked[:, 1]) > near * parts

    k1, fetched = fetch(
        jnp.maximum(blocks_asked, 0),
        owner_at[:near],
        cache.reshape(blocks_dev, BLOCK, width),
        near,
        parts,
    )
    far_shape = (parts, places - near, BLOCK, width)

    def gather_far(x):
        x = x.transpose(1, 0, 2, 3).reshape(seq_count, BLOCK, width)
        return lax.all_gather(take_blocks(owner_at[near:], x), "head", axis=0, tiled=False)

    k2 = lax.cond(overflow, gather_far, lambda x: unset(x, far_shape), fetched)
    out, d_queries, dk1, dk2 = attend(
        count[None], slots, q_pos % BLOCK, queries, d_out, k1, k2
    )
    r2 = lax.cond(
        overflow,
        lambda x: lax.psum_scatter(x, "head", scatter_dimension=0, tiled=False),
        lambda x: unset(x, far_shape[1:]),
        dk2,
    )
    returned = give_back(place_of, dk1, r2)
    owned = add_blocks(blocks_asked, returned, blocks_dev)
    d_cache = widen_turned(
        lax.psum_scatter(
            owned.reshape(blocks_dev * BLOCK, width), "head", scatter_dimension=0, tiled=True
        )
    )
    return (out, d_queries, d_cache)


def solution(mesh):
    placed = (
        P("seq", "head", None),
        P("seq", None),
        P("seq", "head", None),
        P("seq", None),
        P("seq"),
    )
    return jax.shard_map(
        on_device,
        mesh=mesh,
        in_specs=placed,
        out_specs=(P("seq", "head", None), P("seq", "head", None), P(("seq", "head"), None)),
        check_vma=False,
    )
```
